128 devices in a mesh: fsdp: 128 (over x, y, z, core).
Axes of the slice: x: 4, y: 4, z: 4, core: 2. Of those that a mesh axis runs over, the one named last changes fastest.
Arguments:
- tokens: bfloat16 [16384, 1024], P('fsdp'), may hold values from -6 to 6
- norm_gain: bfloat16 [1024], P('fsdp'), may hold values from 0.25 to 1.75
- in_weight: bfloat16 [1024, 3072], P('fsdp'), may hold values from -0.1875 to 0.1875
- conv_weight: bfloat16 [3, 1024], P(None, 'fsdp'), may hold values from -3.5 to 3.5
- out_weight: bfloat16 [1024, 1024], P('fsdp'), may hold values from -0.1875 to 0.1875
- ffn_gain: bfloat16 [1024], P('fsdp'), may hold values from 0.25 to 1.75
- gate_weight: bfloat16 [1024, 4608], P('fsdp'), may hold values from -0.1875 to 0.1875
- up_weight: bfloat16 [1024, 4608], P('fsdp'), may hold values from -0.1875 to 0.1875
- down_weight: bfloat16 [4608, 1024], P('fsdp'), may hold values from -0.1875 to 0.1875
- seq_start: int32 [128], replicated, may hold values from 0 to 128, as said below
- out_grad: bfloat16 [16384, 1024], P('fsdp'), may hold values from -6 to 6
Outputs:
- block_output: bfloat16 [16384, 1024], P('fsdp')
- tokens_grad: bfloat16 [16384, 1024], P('fsdp')
- norm_gain_grad: float32 [1024], P('fsdp')
- in_weight_grad: float32 [1024, 3072], P('fsdp')
- conv_weight_grad: float32 [3, 1024], P(None, 'fsdp')
- out_weight_grad: float32 [1024, 1024], P('fsdp')
- ffn_gain_grad: float32 [1024], P('fsdp')
- gate_weight_grad: float32 [1024, 4608], P('fsdp')
- up_weight_grad: float32 [1024, 4608], P('fsdp')
- down_weight_grad: float32 [4608, 1024], P('fsdp')
The draws below stay inside these ranges and needn't reach their ends.
Inputs may be any that keep to these rules, and one draw needn't show every extreme that they name: `seq_start`: 128 stands for no document beginning in the block. Block 0 holds 0; every other block whose index is a multiple of 16 holds an offset of 2 or more; all other blocks hold 128.
All inputs are finite; a program needn't handle non-finite values.
Results may differ from the reference program's by a relative error of at most 0.011.
Values may be sent and summed in bfloat16 or wider, within the bound.
No kernel may reach another device: no remote copies, remote signals or barrier semaphores. Data moves between devices by JAX's collectives and lax.ppermute only.
A program may use at most 192 MiB of HBM per device.

```python
import math
import jax
import jax.numpy as jnp
from jax import lax

D = 1024
FF = 4608
TOK_DEV = 128
SEQ_BLOCKS = 16
TOKENS = 16384
N_FSDP = 128


def draw_seq_start(key, part):
    key = jax.random.fold_in(key, 7)
    offsets = jax.random.randint(key, (N_FSDP,), 2, TOK_DEV).astype(jnp.int32)
    blocks = jnp.arange(N_FSDP, dtype=jnp.int32)
    chosen = jnp.where(blocks % SEQ_BLOCKS == 0, offsets, TOK_DEV)
    return jnp.where(blocks == 0, 0, chosen).astype(jnp.int32)


def levels(stream_key, extent, pieces, least, largest):
    level = 1.0
    for dim, parts in pieces:
        steps = jax.random.uniform(jax.random.fold_in(jax.random.fold_in(stream_key, 6), dim), (parts,), jnp.float32, least / len(pieces), largest / len(pieces))
        level = level * jnp.repeat(jnp.exp(steps), extent[dim] // parts).reshape((-1,) + (1,) * (len(extent) - 1 - dim))
    return level


def noise(key, shape, width, most, split=(), held_as=jnp.bfloat16):
    level = levels(key, shape, split, -0.22, 0.18) if split else 1.0
    drawn = jax.random.normal(key, shape, jnp.float32) * width * level
    return jnp.minimum(jnp.maximum(drawn, -most), most).astype(held_as)


def setup_inputs(seed: int = 0) -> dict:
    key_list = jax.random.split(jax.random.key(seed), 12)
    tokens = noise(key_list[0], (TOKENS, D), 1.0, 6.0, ((0, 128),))
    norm_gain = jnp.clip(1.0 + 0.15 * jax.random.normal(key_list[1], (D,), jnp.float32), 0.25, 1.75).astype(jnp.bfloat16)
    in_weight = noise(key_list[2], (D, 3 * D), D ** -0.5, 0.1875, ((0, 128),))
    conv_weight = noise(key_list[3], (3, D), 3 ** -0.5, 3.5, ((1, 128),))
    out_weight = noise(key_list[4], (D, D), D ** -0.5, 0.1875, ((0, 128),))
    ffn_gain = jnp.clip(1.0 + 0.15 * jax.random.normal(key_list[5], (D,), jnp.float32), 0.25, 1.75).astype(jnp.bfloat16)
    gate_weight = noise(key_list[6], (D, FF), D ** -0.5, 0.1875, ((0, 128),))
    up_weight = noise(key_list[7], (D, FF), D ** -0.5, 0.1875, ((0, 128),))
    down_weight = noise(key_list[8], (FF, D), (FF // 4) ** -0.5, 0.1875, ((0, 128),))
    seq_start = draw_seq_start(jax.random.fold_in(key_list[11], 71), 0)
    out_grad = noise(key_list[10], (TOKENS, D), 1.0, 6.0, ((0, 128),))
    return dict(tokens=tokens, norm_gain=norm_gain, in_weight=in_weight, conv_weight=conv_weight, out_weight=out_weight, ffn_gain=ffn_gain, gate_weight=gate_weight, up_weight=up_weight, down_weight=down_weight, seq_start=seq_start, out_grad=out_grad)


EPS = 1e-05

@jax.custom_vjp
def low(v):
    return lax.optimization_barrier(v.astype(jnp.bfloat16)).astype(jnp.float32)

@jax.custom_vjp
def low_back(v):
    return v

def low_keep(v):
    return (low(v), None)

def low_pass(kept, grad):
    return (grad,)

def back_keep(v):
    return (v, None)

def back_low(kept, grad):
    return (low(grad),)
low.defvjp(low_keep, low_pass)
low_back.defvjp(back_keep, back_low)

def matmul(left, right):
    return jnp.dot(left, right, precision=lax.Precision.HIGHEST, preferred_element_type=jnp.float32)

def rms_scale(values, gain):
    return values * lax.rsqrt(lax.optimization_barrier(jnp.mean(values * values, axis=-1, keepdims=True)) + EPS) * gain

def lag_masks(seq_start):
    blocks = jnp.arange(N_FSDP, dtype=jnp.int32)
    starts = jnp.where(seq_start < TOK_DEV, blocks * TOK_DEV + seq_start, TOKENS).astype(jnp.int32)
    places = jnp.arange(TOKENS, dtype=jnp.int32)
    segment = lax.optimization_barrier(jnp.sum((starts[None, :] <= places[:, None]).astype(jnp.int32), axis=1))
    first = (segment[1:] == segment[:-1]).astype(jnp.int32)
    second = (segment[2:] == segment[:-2]).astype(jnp.int32)
    lag_one = jnp.concatenate([jnp.zeros((1,), jnp.int32), first])
    lag_two = jnp.concatenate([jnp.zeros((2,), jnp.int32), second])
    return (lag_one.astype(jnp.float32), lag_two.astype(jnp.float32))

def layer_forward(hidden, gain_one, in_proj, conv_taps, out_proj, gain_two, gate_proj, up_proj, down_proj, lag_one, lag_two):
    block_rows = math.gcd(TOKENS, 4096)
    block_count = TOKENS // block_rows

    def block(edge_rows, inputs):
        tok_rows, one_mask, two_mask = inputs
        normed = low(rms_scale(tok_rows, gain_one))
        projected = low_back(matmul(normed, in_proj))
        b_part = projected[:, :D]
        c_part = projected[:, D:2 * D]
        x_part = projected[:, 2 * D:]
        product = low(b_part * x_part)
        extended = jnp.concatenate([edge_rows, product], axis=0)
        convolved = conv_taps[0] * product + one_mask[:, None] * conv_taps[1] * extended[1:-1] + two_mask[:, None] * conv_taps[2] * extended[:-2]
        gated = low(c_part * convolved)
        branch = low_back(matmul(gated, out_proj))
        middle = tok_rows + branch
        second = low(rms_scale(middle, gain_two))
        gate_value = low_back(matmul(second, gate_proj))
        up_value = low_back(matmul(second, up_proj))
        activated = low(jax.nn.silu(gate_value) * up_value)
        output = middle + matmul(activated, down_proj)
        return (product[-2:], output)
    start_rows = jnp.zeros((2, D), jnp.float32)
    inputs = (hidden.reshape(block_count, block_rows, D), lag_one.reshape(block_count, block_rows), lag_two.reshape(block_count, block_rows))
    unused, outputs = lax.scan(jax.checkpoint(block), start_rows, inputs)
    return outputs.reshape(TOKENS, D)

def widen(array):
    return array.astype(jnp.float32)

def reference(tokens, norm_gain, in_weight, conv_weight, out_weight, ffn_gain, gate_weight, up_weight, down_weight, seq_start, out_grad):
    lag_one, lag_two = lag_masks(seq_start)
    params = (widen(tokens), widen(norm_gain), widen(in_weight), widen(conv_weight), widen(out_weight), widen(ffn_gain), widen(gate_weight), widen(up_weight), widen(down_weight))

    def forward(hidden, gain_one, in_proj, conv_taps, out_proj, gain_two, gate_proj, up_proj, down_proj):
        return layer_forward(hidden, gain_one, in_proj, conv_taps, out_proj, gain_two, gate_proj, up_proj, down_proj, lag_one, lag_two)
    output, pullback = jax.vjp(forward, *params)
    gradients = pullback(widen(out_grad))
    return (output.astype(jnp.bfloat16), gradients[0].astype(jnp.bfloat16), gradients[1], gradients[2], gradients[3], gradients[4], gradients[5], gradients[6], gradients[7], gradients[8])
```

```python
import jax
import jax.numpy as jnp
from jax import lax
from jax.sharding import PartitionSpec as P

EPS = 1e-05
AXES = {"x": 5, "y": 3, "z": 1}
DIM = {"x": 0, "y": 1, "z": 2}
BF = jnp.bfloat16
F32 = jnp.float32


def contract(left, right, left_dim, right_dim):
    return lax.dot_general(
        left, right, (((left_dim,), (right_dim,)), ((), ())), preferred_element_type=F32
    )


def swap_core(value):
    return lax.ppermute(value, "fsdp", [(d, d ^ 1) for d in range(128)])


def swap_chip(value, axis, masks):
    low = AXES[axis]
    return lax.ppermute(value, "fsdp", [(d, d ^ (masks[d & 1] << low)) for d in range(128)])


def next_chip(value, by):
    return lax.ppermute(
        value, "fsdp", [(d, d + 2 * by) for d in range(128) if 0 <= d + 2 * by < 128]
    )


class Place:
    def __init__(self):
        device = lax.axis_index("fsdp")
        self.device = device
        self.core = device & 1
        self.chip = device >> 1
        self.at = {axis: (device >> low) & 3 for axis, low in AXES.items()}


def by_core(core, mine, other, axis):
    first = jnp.where(core == 0, mine, other)
    second = jnp.where(core == 0, other, mine)
    return jnp.concatenate([first, second], axis=axis)


def gather_axis(place, block, axis, dim):
    near = swap_chip(block, axis, (1, 3))
    pair = jnp.stack([block, near])
    far = swap_chip(pair, axis, (3, 1))
    me = place.at[axis]
    shape = block.shape[:dim] + (4,) + block.shape[dim:]
    out = jnp.zeros(shape, block.dtype)
    one = jnp.where(place.core == 0, 1, 3)
    for code, part in ((0, block), (one, near), (4 - one, far[0]), (2, far[1])):
        where = [jnp.int32(0)] * len(shape)
        where[dim] = me ^ code
        out = lax.dynamic_update_slice(out, jnp.expand_dims(part, dim), where)
    return out


def scatter_axis(place, terms, axis, dim):
    me = place.at[axis]
    one = jnp.where(place.core == 0, 3, 1)
    two = 4 - one

    def take(code):
        return lax.dynamic_index_in_dim(terms, me ^ code, dim, keepdims=False)

    far = swap_chip(jnp.stack([take(one), take(2)]), axis, (3, 1))
    passing = (take(two).astype(F32) + far[1].astype(F32)).astype(BF)
    near = swap_chip(passing, axis, (1, 3))
    return take(jnp.int32(0)).astype(F32) + far[0].astype(F32) + near.astype(F32)


def inverse_rms(values):
    return lax.rsqrt(jnp.mean(values * values, axis=-1, keepdims=True) + EPS)


def norm_backward(scaled, inverse, gain, upstream):
    inner = upstream * gain
    return inverse * (inner - scaled * jnp.mean(inner * scaled, axis=-1, keepdims=True))


def halves(array):
    mid = array.shape[-1] // 2
    return (array[..., :mid], array[..., mid:])


def on_device(
    tokens,
    norm_gain,
    in_weight,
    conv_weight,
    out_weight,
    ffn_gain,
    gate_weight,
    up_weight,
    down_weight,
    seq_start,
    out_grad,
):
    place = Place()
    core = place.core
    length = tokens.shape[0]
    rows = 2 * length
    d_model = tokens.shape[1]
    half = d_model // 2
    quarter = half // 2
    ff = gate_weight.shape[1]
    ff_half = ff // 2
    side = 3 * quarter

    both = jnp.stack([tokens, out_grad])
    both = by_core(core, both, swap_core(both), 1)
    tok, grad_out = both[0], both[1]

    b_w, c_w, x_w = (halves(in_weight[:, i * d_model : (i + 1) * d_model]) for i in range(3))
    gate_w, up_w, out_w, down_w = (
        halves(w) for w in (gate_weight, up_weight, out_weight, down_weight)
    )
    small = jnp.concatenate([norm_gain[:, None], conv_weight.T, ffn_gain[:, None]], axis=1)
    small = jnp.pad(small, ((0, 0), (0, 123)))
    lanes = [
        jnp.concatenate(
            [b_w[h], c_w[h][:, :quarter], small, gate_w[h], c_w[h][:, quarter:], x_w[h], up_w[h], out_w[h]],
            axis=1,
        )
        for h in range(2)
    ]
    mine = jnp.where(core == 0, lanes[0], lanes[1])
    yours = jnp.where(core == 0, lanes[1], lanes[0])
    wide = by_core(core, mine, swap_core(yours), 0)
    down_mine = jnp.where(core == 0, down_w[0], down_w[1])
    down_yours = jnp.where(core == 0, down_w[1], down_w[0])
    down_rows = by_core(core, down_mine, swap_core(down_yours), 0)
    cut_a = side + 128 + ff_half
    cut_b = cut_a + side + ff_half
    flow_a = wide[:, :cut_a]
    flow_b = wide[:, cut_a:cut_b]
    flow_c = jnp.concatenate([wide[:, cut_b:], down_rows], axis=0)
    own_rows = wide.shape[0]

    flow_a = gather_axis(place, flow_a, "x", 0)
    flow_b = gather_axis(place, flow_b, "y", 0)
    flow_c = gather_axis(place, flow_c, "z", 0)
    flow_a = gather_axis(place, flow_a, "y", 1)
    flow_b = gather_axis(place, flow_b, "z", 1)
    flow_c = gather_axis(place, flow_c, "x", 0)
    mix_a = gather_axis(place, flow_a[..., : side + 128], "z", 2).reshape(d_model, side + 128)
    mix_b = gather_axis(place, flow_b[..., :side], "x", 0).reshape(d_model, side)
    mix_c = gather_axis(place, flow_c[:, :, :own_rows], "y", 1).reshape(d_model, half)
    gate_c = gather_axis(place, flow_a[..., side + 128 :], "z", 2).reshape(d_model, ff_half)
    up_c = gather_axis(place, flow_b[..., side:], "x", 0).reshape(d_model, ff_half)
    down_cols = gather_axis(place, flow_c[:, :, own_rows:], "y", 1).reshape(ff, half)

    in_a, in_b = mix_a[:, :side], mix_b
    smalls = mix_a[:, side:].T[:8].astype(F32)
    gain_first, gain_second = smalls[0], smalls[4]
    taps = lax.dynamic_slice(smalls, (1, core * half), (3, half))
    out_full = by_core(core, mix_c, swap_core(mix_c), 1)

    offsets = jnp.arange(rows, dtype=jnp.int32)
    first_block = 2 * place.chip
    before = lax.dynamic_index_in_dim(seq_start, jnp.maximum(first_block - 1, 0), 0, keepdims=False)
    start_0 = lax.dynamic_index_in_dim(seq_start, first_block, 0, keepdims=False)
    start_1 = lax.dynamic_index_in_dim(seq_start, first_block + 1, 0, keepdims=False)
    begin_0 = jnp.where(start_0 < length, start_0, -9)
    begin_1 = jnp.where(start_1 < length, start_1 + length, -9)
    begin_p = jnp.where((before == length - 1) & (first_block > 0), -1, -9)

    def begins(at):
        return (at == begin_0) | (at == begin_1) | (at == begin_p)

    lag_one = jnp.where(begins(offsets), 0.0, 1.0).astype(F32)[:, None]
    lag_two = jnp.where(begins(offsets) | begins(offsets - 1), 0.0, 1.0).astype(F32)[:, None]

    hidden = tok.astype(F32)
    inverse_one = inverse_rms(hidden)
    scaled_one = hidden * inverse_one
    normed = (scaled_one * gain_first).astype(BF)
    proj_a = jnp.dot(normed, in_a, preferred_element_type=F32)
    proj_b = jnp.dot(normed, in_b, preferred_element_type=F32)
    b_part, x_part = proj_a[:, :half], proj_b[:, quarter:]
    c_part = jnp.concatenate([proj_a[:, half:], proj_b[:, :quarter]], axis=1)
    product = (b_part * x_part).astype(BF)
    edge = next_chip(product[rows - 2 :], 1)
    extended = jnp.concatenate([edge, product], axis=0).astype(F32)
    lagged_one = lag_one * extended[1:-1]
    lagged_two = lag_two * extended[:-2]
    convolved = taps[0] * extended[2:] + taps[1] * lagged_one + taps[2] * lagged_two
    gated = (c_part * convolved).astype(BF)
    gated_full = by_core(core, gated, swap_core(gated), 1)
    middle = hidden + jnp.dot(gated_full, out_full, preferred_element_type=F32)

    inverse_two = inverse_rms(middle)
    scaled_two = middle * inverse_two
    second = (scaled_two * gain_second).astype(BF)
    gate_value = jnp.dot(second, gate_c, preferred_element_type=F32)
    up_value = jnp.dot(second, up_c, preferred_element_type=F32)
    gate_sigmoid = jax.nn.sigmoid(gate_value)
    gate_silu = gate_value * gate_sigmoid
    activated = (gate_silu * up_value).astype(BF)
    grad_own = lax.dynamic_slice(grad_out, (0, core * half), (rows, half))
    grad_far = lax.dynamic_slice(grad_out, (0, (1 - core) * half), (rows, half))
    down_grad_own = contract(activated, grad_own, 0, 0).astype(BF)
    down_grad_far = contract(activated, grad_far, 0, 0).astype(BF)
    down_own = lax.dynamic_slice(down_cols, (core * ff_half, 0), (ff_half, half))
    down_far = swap_core(lax.dynamic_slice(down_cols, ((1 - core) * ff_half, 0), (ff_half, half)))
    act_grad = contract(grad_own, down_own, 1, 1) + contract(grad_far, down_far, 1, 1)
    gate_grad = (
        act_grad * up_value * gate_sigmoid * (1.0 + gate_value * (1.0 - gate_sigmoid))
    ).astype(BF)
    up_grad = (act_grad * gate_silu).astype(BF)
    second_part = contract(gate_grad, gate_c, 1, 1) + contract(up_grad, up_c, 1, 1)
    second_grad = second_part + swap_core(second_part)

    gate_terms = contract(second, gate_grad, 0, 0).astype(BF).reshape(4, 4, 4, own_rows, ff_half)
    up_terms = contract(second, up_grad, 0, 0).astype(BF).reshape(4, 4, 4, own_rows, ff_half)
    down_terms = by_core(core, down_grad_own, swap_core(down_grad_far), 0)
    down_terms = down_terms.reshape(4, 4, 4, ff // 64, half)
    gate_sum = scatter_axis(place, gate_terms, "z", 2).astype(BF)
    up_sum = scatter_axis(place, up_terms, "x", 0).astype(BF)
    down_sum = scatter_axis(place, down_terms, "y", 1).astype(BF)

    out_own = jnp.dot(activated, down_own, preferred_element_type=F32)
    out_far = jnp.dot(activated, down_far, preferred_element_type=F32)
    out_part = by_core(core, out_own, out_far, 1)
    got = swap_core(lax.dynamic_slice(out_part, ((1 - core) * length, 0), (length, d_model)))
    own_at = (core * length, 0)
    block_output = (
        lax.dynamic_slice(middle, own_at, (length, d_model))
        + lax.dynamic_slice(out_part, own_at, (length, d_model))
        + got
    ).astype(BF)

    middle_grad = grad_out.astype(F32) + norm_backward(
        scaled_two, inverse_two, gain_second, second_grad
    )
    gain_two_grad = jnp.sum(second_grad * scaled_two, axis=0) * (core == 0).astype(F32)
    branch_grad = middle_grad.astype(BF)
    out_rows = lax.dynamic_slice(out_full, (core * half, 0), (half, d_model))
    gated_grad = contract(branch_grad, out_rows, 1, 1)
    out_terms = contract(
        gated_full, lax.dynamic_slice(branch_grad, (0, core * half), (rows, half)), 0, 0
    ).astype(BF)
    convolved_grad = gated_grad * c_part
    c_grad = gated_grad * convolved
    from_one = taps[1] * lag_one * convolved_grad
    from_two = taps[2] * lag_two * convolved_grad
    spread = jnp.pad(from_one, ((1, 1), (0, 0))) + jnp.pad(from_two, ((0, 2), (0, 0)))
    returned = next_chip(spread[:2], -1)
    product_grad = (
        taps[0] * convolved_grad + spread[2:] + jnp.pad(returned, ((rows - 2, 0), (0, 0)))
    )
    tap_grads = jnp.stack(
        [
            jnp.sum(convolved_grad * extended[2:], axis=0),
            jnp.sum(convolved_grad * lagged_one, axis=0),
            jnp.sum(convolved_grad * lagged_two, axis=0),
        ]
    )
    c_grad = c_grad.astype(BF)
    grad_a = jnp.concatenate([(product_grad * x_part).astype(BF), c_grad[:, :quarter]], axis=1)
    grad_b = jnp.concatenate([c_grad[:, quarter:], (product_grad * b_part).astype(BF)], axis=1)
    normed_part = contract(grad_a, in_a, 1, 1) + contract(grad_b, in_b, 1, 1)
    gain_one_grad = jnp.sum(normed_part * scaled_one, axis=0)
    tap_full = lax.dynamic_update_slice(
        jnp.zeros((3, d_model), F32), tap_grads, (0, core * half)
    )
    extra = jnp.concatenate(
        [gain_one_grad[None], tap_full, gain_two_grad[None], jnp.zeros((123, d_model), F32)]
    ).T.astype(BF)
    terms_a = jnp.concatenate([contract(normed, grad_a, 0, 0).astype(BF), extra], axis=1)
    terms_b = contract(normed, grad_b, 0, 0).astype(BF)
    mix_a = scatter_axis(place, terms_a.reshape(4, 4, 4, own_rows, -1), "z", 2).astype(BF)
    mix_b = scatter_axis(place, terms_b.reshape(4, 4, 4, own_rows, -1), "x", 0).astype(BF)
    mix_c = scatter_axis(place, out_terms.reshape(4, 4, 4, own_rows, -1), "y", 1).astype(BF)

    got = swap_core(lax.dynamic_slice(normed_part, ((1 - core) * length, 0), (length, d_model)))
    normed_grad = lax.dynamic_slice(normed_part, own_at, (length, d_model)) + got
    tokens_grad = (
        lax.dynamic_slice(middle_grad, own_at, (length, d_model))
        + norm_backward(
            lax.dynamic_slice(scaled_one, own_at, (length, d_model)),
            lax.dynamic_slice(inverse_one, own_at, (length, 1)),
            gain_first,
            normed_grad,
        )
    ).astype(BF)

    flow_a = jnp.concatenate([mix_a, gate_sum], axis=-1)
    flow_b = jnp.concatenate([mix_b, up_sum], axis=-1)
    flow_c = jnp.concatenate([mix_c, down_sum], axis=-2)
    flow_a = scatter_axis(place, flow_a, "y", 1).astype(BF)
    flow_b = scatter_axis(place, flow_b, "z", 1).astype(BF)
    flow_c = scatter_axis(place, flow_c, "x", 0).astype(BF)
    flow_a = scatter_axis(place, flow_a, "x", 0)
    flow_b = scatter_axis(place, flow_b, "y", 0)
    flow_c = scatter_axis(place, flow_c, "z", 0)

    wide = jnp.concatenate([flow_a, flow_b, flow_c[:own_rows]], axis=1)
    lead = own_rows // 2
    mine = jnp.where(core == 0, wide[:lead], wide[lead:])
    got = swap_core(jnp.where(core == 0, wide[lead:], wide[:lead]))
    down_rows = flow_c[own_rows:]
    deep = down_rows.shape[0] // 2
    down_mine = jnp.where(core == 0, down_rows[:deep], down_rows[deep:])
    down_got = swap_core(jnp.where(core == 0, down_rows[deep:], down_rows[:deep]))
    zero = jnp.where(core == 0, mine, got)
    one = jnp.where(core == 0, got, mine)

    def joined(start, stop):
        return [zero[:, start:stop], one[:, start:stop]]

    b_cols = joined(0, half)
    c_cols = [
        jnp.concatenate([h[:, half:side], h[:, cut_a : cut_a + quarter]], axis=1)
        for h in (zero, one)
    ]
    x_cols = joined(cut_a + quarter, cut_a + side)
    in_weight_grad = jnp.concatenate(b_cols + c_cols + x_cols, axis=1)
    gate_weight_grad = jnp.concatenate(joined(side + 128, cut_a), axis=1)
    up_weight_grad = jnp.concatenate(joined(cut_a + side, cut_b), axis=1)
    out_weight_grad = jnp.concatenate(joined(cut_b, cut_b + half), axis=1)
    down_weight_grad = by_core(core, down_mine, down_got, 1)
    small = (mine[:, side : side + 8] + got[:, side : side + 8]).T
    return (
        block_output,
        tokens_grad,
        small[0],
        in_weight_grad,
        small[1:4],
        out_weight_grad,
        small[4],
        gate_weight_grad,
        up_weight_grad,
        down_weight_grad,
    )


def solution(mesh):
    return jax.shard_map(
        on_device,
        mesh=mesh,
        in_specs=(
            P("fsdp", None),
            P("fsdp"),
            P("fsdp", None),
            P(None, "fsdp"),
            P("fsdp", None),
            P("fsdp"),
            P("fsdp", None),
            P("fsdp", None),
            P("fsdp", None),
            P(),
            P("fsdp", None),
        ),
        out_specs=(
            P("fsdp", None),
            P("fsdp", None),
            P("fsdp"),
            P("fsdp", None),
            P(None, "fsdp"),
            P("fsdp", None),
            P("fsdp"),
            P("fsdp", None),
            P("fsdp", None),
            P("fsdp", None),
        ),
        check_vma=False,
    )
```

```python
import jax
import jax.numpy as jnp
from jax import lax
from jax.experimental import pallas as pl
from jax.experimental.pallas import tpu as pltpu
from jax.sharding import PartitionSpec as P

EPS = 1e-05
AXES = {"x": 5, "y": 3, "z": 1}
DIM = {"x": 0, "y": 1, "z": 2}
BF = jnp.bfloat16
F32 = jnp.float32


def contract(left, right, left_dim, right_dim):
    return lax.dot_general(
        left, right, (((left_dim,), (right_dim,)), ((), ())), preferred_element_type=F32
    )


def swap_core(value):
    return lax.ppermute(value, "fsdp", [(d, d ^ 1) for d in range(128)])


def swap_chip(value, axis, masks):
    low = AXES[axis]
    return lax.ppermute(value, "fsdp", [(d, d ^ (masks[d & 1] << low)) for d in range(128)])


def next_chip(value, by):
    return lax.ppermute(
        value, "fsdp", [(d, d + 2 * by) for d in range(128) if 0 <= d + 2 * by < 128]
    )


class Place:
    def __init__(self):
        device = lax.axis_index("fsdp")
        self.device = device
        self.core = device & 1
        self.chip = device >> 1
        self.at = {axis: (device >> low) & 3 for axis, low in AXES.items()}


def by_core(core, mine, other, axis):
    first = jnp.where(core == 0, mine, other)
    second = jnp.where(core == 0, other, mine)
    return jnp.concatenate([first, second], axis=axis)


def after(value, *before):
    return lax.optimization_barrier((value, *before))[0]


def arrange(core, pairs, half, ff_half):
    quarter = half // 2
    rows = 2 * pairs[0].shape[0]
    deep = 2 * pairs[8].shape[0]

    def kernel(core_ref, *refs):
        ins, (flow_a, flow_b, flow_c) = refs[:12], refs[12:]

        def columns(which, start, width, step):
            mine, other = ins[2 * which], ins[2 * which + 1]
            zero = [mine[:, start : start + width], other[:, start : start + width]]
            start += step
            one = [other[:, start : start + width], mine[:, start : start + width]]
            picked = [
                jnp.where(core_ref[0] == 0, z.astype(F32), o.astype(F32)) for z, o in zip(zero, one)
            ]
            return jnp.concatenate(picked, axis=0)

        def upright(zero, one):
            vectors = jnp.where(core_ref[0] == 0, zero[...].astype(F32), one[...].astype(F32))
            square = jnp.concatenate([vectors, jnp.zeros((120, 128), F32)], axis=0)
            return square.T[:8]

        flow_a[:, :half] = columns(0, 0, half, half).astype(BF)
        flow_a[:, half : half + quarter] = columns(0, 2 * half, quarter, half).astype(BF)
        flow_a[:, half + quarter : half + quarter + 128] = jnp.concatenate(
            [upright(ins[10], ins[11]), upright(ins[11], ins[10])], axis=0
        ).astype(BF)
        flow_a[:, half + quarter + 128 :] = columns(1, 0, ff_half, ff_half).astype(BF)
        flow_b[:, :quarter] = columns(0, 2 * half + quarter, quarter, half).astype(BF)
        flow_b[:, quarter : quarter + half] = columns(0, 4 * half, half, half).astype(BF)
        flow_b[:, half + quarter :] = columns(2, 0, ff_half, ff_half).astype(BF)
        last = [columns(3, 0, half, half), columns(4, 0, half, half)]
        flow_c[...] = jnp.concatenate(last, axis=0).astype(BF)

    vmem = pl.BlockSpec(memory_space=pltpu.VMEM)
    wide_a = jax.ShapeDtypeStruct((rows, half + quarter + 128 + ff_half), BF)
    wide_b = jax.ShapeDtypeStruct((rows, half + quarter + ff_half), BF)
    return pl.pallas_call(
        kernel,
        out_shape=[wide_a, wide_b, jax.ShapeDtypeStruct((rows + deep, half), BF)],
        in_specs=[pl.BlockSpec(memory_space=pltpu.SMEM)] + [vmem] * 12,
        out_specs=[vmem] * 3,
        name="arrange",
    )(core.reshape(1), *pairs)


def finish(core, arrays, half, ff_half):
    quarter = half // 2
    side = half + quarter
    few = arrays[3].shape[0]
    deep = arrays[6].shape[0]

    def kernel(core_ref, *refs):
        flow_a, flow_b, flow_c, got_a, got_b, got_out, got_down = refs[:7]
        in_grad, gate_grad, up_grad, out_grad, down_grad, norm_grad, tap_grad, ffn_norm_grad = refs[7:]
        first = core_ref[0] == 0

        def own(flow, start, count, lanes):
            return jnp.where(
                first, flow[start : start + count, lanes], flow[start + count : start + 2 * count, lanes]
            )

        def both(ref, at, mine, other):
            width = mine.shape[1]
            ref[:, at : at + width] = jnp.where(first, mine, other)
            at += ref.shape[1] // 2 if ref is not in_grad else half
            ref[:, at : at + width] = jnp.where(first, other, mine)

        def rows(flow, got, at, lanes, ref):
            both(ref, at, own(flow, 0, few, lanes), got[:, lanes])

        rows(flow_a, got_a, 0, slice(0, half), in_grad)
        rows(flow_a, got_a, 2 * half, slice(half, side), in_grad)
        rows(flow_b, got_b, 2 * half + quarter, slice(0, quarter), in_grad)
        rows(flow_b, got_b, 4 * half, slice(quarter, side), in_grad)
        rows(flow_a, got_a, 0, slice(side + 128, side + 128 + ff_half), gate_grad)
        rows(flow_b, got_b, 0, slice(side, side + ff_half), up_grad)
        rows(flow_c, got_out, 0, slice(0, half), out_grad)
        both(down_grad, 0, own(flow_c, 2 * few, deep, slice(0, half)), got_down[...])
        lanes = slice(side, side + 128)
        vectors = own(flow_a, 0, few, lanes) + got_a[:, lanes]
        square = jnp.concatenate([vectors, jnp.zeros((128 - few, 128), F32)], axis=0)
        square = square.T[:, :few]
        norm_grad[...] = square[0]
        tap_grad[...] = square[1:4]
        ffn_norm_grad[...] = square[4]

    vmem = pl.BlockSpec(memory_space=pltpu.VMEM)
    shapes = [(few, 6 * half), (few, 2 * ff_half), (few, 2 * ff_half), (few, 2 * half), (deep, 2 * half)]
    shapes += [(few,), (3, few), (few,)]
    return pl.pallas_call(
        kernel,
        out_shape=[jax.ShapeDtypeStruct(shape, F32) for shape in shapes],
        in_specs=[pl.BlockSpec(memory_space=pltpu.SMEM)] + [vmem] * 7,
        out_specs=[vmem] * 8,
        name="finish",
    )(core.reshape(1), *arrays)


def put(place, parts, axis, dim):
    block = parts[0][1]
    me = place.at[axis]
    shape = block.shape[:dim] + (4,) + block.shape[dim:]
    out = jnp.zeros(shape, block.dtype)
    for code, part in parts:
        where = [jnp.int32(0)] * len(shape)
        where[dim] = me ^ code
        out = lax.dynamic_update_slice(out, jnp.expand_dims(part, dim), where)
    return out


def gather_far(place, block, near, axis, dim):
    sent = jnp.stack([block, near])
    far = swap_chip(sent, axis, (3, 1))
    one = jnp.where(place.core == 0, 1, 3)
    return put(place, ((0, block), (one, near), (4 - one, far[0]), (2, far[1])), axis, dim), sent


def gather_axis(place, block, axis, dim):
    return gather_far(place, block, swap_chip(block, axis, (1, 3)), axis, dim)[0]


def scatter_far(place, terms, axis, dim):
    me = place.at[axis]
    one = jnp.where(place.core == 0, 3, 1)

    def take(code):
        if isinstance(terms, list):
            return jnp.stack(
                [lax.dynamic_index_in_dim(t, me ^ code, dim, keepdims=False) for t in terms]
            )
        return lax.dynamic_index_in_dim(terms, me ^ code, dim, keepdims=False)

    sent = jnp.stack([take(one), take(2)])
    return swap_chip(sent, axis, (3, 1)), take(4 - one), take(jnp.int32(0)), sent


def block_order(place, axis):
    spot = jnp.arange(1024, dtype=jnp.int32)
    one = jnp.where(place.core == 0, 1, 3)
    which = spot >> 8
    code = jnp.where(which == 0, 0, jnp.where(which == 1, one, jnp.where(which == 2, 4 - one, 2)))
    there = place.at[axis] ^ code
    high, low, inner = (spot >> 6) & 3, (spot >> 4) & 3, spot & 15
    x, y, z = {"x": (there, high, low), "y": (high, there, low), "z": (high, low, there)}[axis]
    source = x * 256 + y * 64 + z * 16 + inner
    return (source[:, None] == spot[None, :]).astype(BF)


def scatter_dot(order, left, right, axis, extra=None):
    left = contract(order, left, 1, 1).astype(BF)
    if extra is not None:
        extra = contract(order, extra, 1, 1).astype(BF)

    def terms(part):
        product = jnp.dot(left[part], right, preferred_element_type=F32).astype(BF)
        if extra is not None:
            product = jnp.concatenate([product, extra[part]], axis=1)
        return product.reshape(2, 4, 4, 16, product.shape[-1])

    sent = terms(slice(512, None))
    keep = terms(slice(None, 512))
    return swap_chip(sent, axis, (3, 1)), keep[1], keep[0], sent


def scatter_pass(half_way):
    far, passing = half_way[:2]
    return (passing.astype(F32) + far[1].astype(F32)).astype(BF)


def scatter_near(far, _, own, __, passing, axis):
    near = swap_chip(passing, axis, (1, 3))
    return own.astype(F32) + far[0].astype(F32) + near.astype(F32)


def scatter_axis(place, terms, axis, dim):
    half_way = scatter_far(place, terms, axis, dim)
    return scatter_near(*half_way, scatter_pass(half_way), axis)


def scatter_small(place, terms, axis):
    total = 0.0
    for code in (1, 3, 2):
        there = lax.dynamic_index_in_dim(terms, place.at[axis] ^ code, 0, keepdims=False)
        total = total + swap_chip(there, axis, (code, code)).astype(F32)
    own = lax.dynamic_index_in_dim(terms, place.at[axis], 0, keepdims=False)
    return total + own.astype(F32)


def inverse_rms(values):
    return lax.rsqrt(jnp.mean(values * values, axis=-1, keepdims=True) + EPS)


def norm_backward(scaled, inverse, gain, upstream):
    inner = upstream * gain
    return inverse * (inner - scaled * jnp.mean(inner * scaled, axis=-1, keepdims=True))


def halves(array):
    mid = array.shape[-1] // 2
    return (array[..., :mid], array[..., mid:])


def on_device(
    tokens,
    norm_gain,
    in_weight,
    conv_weight,
    out_weight,
    ffn_gain,
    gate_weight,
    up_weight,
    down_weight,
    seq_start,
    out_grad,
):
    place = Place()
    core = place.core
    length = tokens.shape[0]
    rows = 2 * length
    d_model = tokens.shape[1]
    half = d_model // 2
    quarter = half // 2
    ff = gate_weight.shape[1]
    ff_half = ff // 2
    side = 3 * quarter

    both = jnp.stack([tokens, out_grad])
    both_other = swap_core(both)
    kinds = jnp.concatenate([norm_gain[None], conv_weight, ffn_gain[None]])
    kinds = jnp.pad(kinds, ((0, 3), (0, 120)))
    shards = [in_weight, gate_weight, up_weight, out_weight, down_weight, kinds]
    pairs = [array for shard in shards for array in (shard, swap_core(shard))]
    both = by_core(core, both, both_other, 1)
    full = rows + 8
    cut_a = side + 128 + ff_half
    cut_b = cut_a + side + ff_half
    flow_a, flow_b, flow_c = arrange(core, pairs, half, ff_half)
    own_rows = 2 * norm_gain.shape[0]

    flow_a = gather_axis(place, flow_a, "x", 0)
    flow_b = gather_axis(place, flow_b, "y", 0)
    flow_c = gather_axis(place, flow_c, "z", 0)
    flow_a = gather_axis(place, flow_a, "y", 1)
    flow_b = gather_axis(place, flow_b, "z", 1)
    flow_c = gather_axis(place, flow_c, "x", 0)
    near_a = swap_chip(flow_a, "z", (1, 3))
    near_b = swap_chip(flow_b, "x", (1, 3))
    near_c = swap_chip(flow_c, "y", (1, 3))
    mix_cut = side + 128

    edges = after((both[:, :2], both[0, rows - 2 :]), flow_a, flow_b, flow_c)
    from_next = next_chip(edges[0], -1)
    from_last = next_chip(edges[1], 1)
    mix_a, sent_a = gather_far(place, flow_a[..., :mix_cut], near_a[..., :mix_cut], "z", 2)
    mix_b, sent_b = gather_far(place, flow_b[..., :side], near_b[..., :side], "x", 0)
    mix_c, sent_c = gather_far(
        place, flow_c[:, :, :own_rows], near_c[:, :, :own_rows], "y", 1
    )
    from_next, from_last = after((from_next, from_last), sent_a, sent_b, sent_c)
    spare = jnp.zeros((4, d_model), BF)
    tok = jnp.concatenate([both[0], from_next[0], from_last, spare])
    grad_out = jnp.concatenate([both[1], from_next[1], from_last * 0, spare])
    flow_a, near_a = after((flow_a[..., mix_cut:], near_a[..., mix_cut:]), sent_a)
    flow_b, near_b = after((flow_b[..., side:], near_b[..., side:]), sent_b)
    flow_c, near_c = after((flow_c[:, :, own_rows:], near_c[:, :, own_rows:]), sent_c)
    gate_c, sent_a = gather_far(place, flow_a, near_a, "z", 2)
    up_c, sent_b = gather_far(place, flow_b, near_b, "x", 0)
    down_cols, sent_c = gather_far(place, flow_c, near_c, "y", 1)
    gate_c, up_c = gate_c.reshape(d_model, ff_half), up_c.reshape(d_model, ff_half)
    down_cols = down_cols.reshape(ff, half)
    mix_a = mix_a.reshape(d_model, mix_cut)
    mix_b = mix_b.reshape(d_model, side)
    mix_c = mix_c.reshape(d_model, half)

    in_a, in_b = mix_a[:, :side], mix_b
    smalls = mix_a[:, side:].T[:8].astype(F32)
    gain_first, gain_second = smalls[0], smalls[4]
    taps = lax.dynamic_slice(smalls, (1, core * half), (3, half))
    out_full = by_core(core, mix_c, swap_core(mix_c), 1)

    offsets = jnp.arange(full, dtype=jnp.int32)
    first_block = 2 * place.chip

    def begin(block, at):
        start = lax.dynamic_index_in_dim(seq_start, jnp.clip(block, 0, 127), 0, keepdims=False)
        there = (start < length) & (block >= 0) & (block < 128)
        return jnp.where(there, start + at, -9)

    begin_at = [begin(first_block + i, i * length) for i in (-1, 0, 1, 2)]

    def begins(at):
        return (at == begin_at[0]) | (at == begin_at[1]) | (at == begin_at[2]) | (at == begin_at[3])

    lag_one = jnp.where(begins(offsets), 0.0, 1.0).astype(F32)[:, None]
    lag_two = jnp.where(begins(offsets) | begins(offsets - 1), 0.0, 1.0).astype(F32)[:, None]

    hidden = tok.astype(F32)
    inverse_one = inverse_rms(hidden)
    scaled_one = hidden * inverse_one
    normed = (scaled_one * gain_first).astype(BF)
    normed = after(normed, sent_a, sent_b, sent_c)
    proj_a = jnp.dot(normed, in_a, preferred_element_type=F32)
    proj_b = jnp.dot(normed, in_b, preferred_element_type=F32)
    b_part, x_part = proj_a[:, :half], proj_b[:, quarter:]
    c_part = jnp.concatenate([proj_a[:, half:], proj_b[:, :quarter]], axis=1)
    wide_product = lax.reduce_precision(b_part * x_part, exponent_bits=8, mantissa_bits=7)
    pad = wide_product[rows + 4 :]
    lagged_one = lag_one * jnp.concatenate(
        [wide_product[rows + 3 : rows + 4], wide_product[: rows + 1], pad, pad[:2]]
    )
    lagged_two = lag_two * jnp.concatenate(
        [wide_product[rows + 2 : rows + 4], wide_product[:rows], pad, pad[:2]]
    )
    convolved = taps[0] * wide_product + taps[1] * lagged_one + taps[2] * lagged_two
    gated = (c_part * convolved).astype(BF)
    gated_full = by_core(core, gated, swap_core(gated), 1)
    middle = hidden + jnp.dot(gated_full, out_full, preferred_element_type=F32)

    inverse_two = inverse_rms(middle)
    scaled_two = middle * inverse_two
    second = (scaled_two * gain_second).astype(BF)
    gate_value = jnp.dot(second, gate_c, preferred_element_type=F32)
    up_value = jnp.dot(second, up_c, preferred_element_type=F32)
    gate_sigmoid = jax.nn.sigmoid(gate_value)
    gate_silu = gate_value * gate_sigmoid
    activated = (gate_silu * up_value).astype(BF)
    grad_own = lax.dynamic_slice(grad_out, (0, core * half), (full, half))
    grad_far = lax.dynamic_slice(grad_out, (0, (1 - core) * half), (full, half))
    activated_far = swap_core(activated[:rows])
    down_own = lax.dynamic_slice(down_cols, (core * ff_half, 0), (ff_half, half))
    down_far = swap_core(lax.dynamic_slice(down_cols, ((1 - core) * ff_half, 0), (ff_half, half)))
    act_grad = contract(grad_own, down_own, 1, 1) + contract(grad_far, down_far, 1, 1)
    gate_grad = (
        act_grad * up_value * gate_sigmoid * (1.0 + gate_value * (1.0 - gate_sigmoid))
    ).astype(BF)
    up_grad = (act_grad * gate_silu).astype(BF)
    down_terms = [
        contract(part, grad_own[:rows], 0, 0).astype(BF).reshape(2, 4, 4, ff // 64, half)
        for part in (activated[:rows], activated_far)
    ]
    down_far_terms = scatter_far(place, down_terms, "y", 1)
    orders = {axis: block_order(place, axis) for axis in AXES}
    gate_far = scatter_dot(orders["z"], after(second[:rows], gate_grad), gate_grad[:rows], "z")
    up_far = scatter_dot(orders["x"], after(second[:rows], up_grad), up_grad[:rows], "x")
    gate_grad, up_grad = after((gate_grad, up_grad), gate_far[3], up_far[3], down_far_terms[3])
    second_part = contract(gate_grad, gate_c, 1, 1) + contract(up_grad, up_c, 1, 1)
    second_grad = second_part + swap_core(second_part)

    own_at = (core * length, 0)
    activated = after(activated[:rows], second_part)
    out_own = jnp.dot(activated, down_own, preferred_element_type=F32)
    out_far = jnp.dot(activated, down_far, preferred_element_type=F32)
    out_part = by_core(core, out_own, out_far, 1)
    got = swap_core(lax.dynamic_slice(out_part, ((1 - core) * length, 0), (length, d_model)))
    block_output = (
        lax.dynamic_slice(middle, own_at, (length, d_model))
        + lax.dynamic_slice(out_part, own_at, (length, d_model))
        + got
    ).astype(BF)

    middle_grad = grad_out.astype(F32) + norm_backward(
        scaled_two, inverse_two, gain_second, second_grad
    )
    gain_two_grad = jnp.sum((second_grad * scaled_two)[:rows], axis=0) * (core == 0).astype(F32)
    branch_grad = middle_grad.astype(BF)
    out_rows = lax.dynamic_slice(out_full, (core * half, 0), (half, d_model))
    gated_grad = contract(branch_grad, out_rows, 1, 1)
    out_right = lax.dynamic_slice(branch_grad, (0, core * half), (rows, half))
    convolved_grad = gated_grad * c_part
    c_grad = gated_grad * convolved
    from_one = taps[1] * lag_one * convolved_grad
    from_two = taps[2] * lag_two * convolved_grad
    convolved_grad, c_grad = convolved_grad[:rows], c_grad[:rows]
    product_grad = taps[0] * convolved_grad + from_one[1 : rows + 1] + from_two[2 : rows + 2]
    tap_grads = jnp.stack(
        [
            jnp.sum(convolved_grad * wide_product[:rows], axis=0),
            jnp.sum(convolved_grad * lagged_one[:rows], axis=0),
            jnp.sum(convolved_grad * lagged_two[:rows], axis=0),
        ]
    )
    c_grad = c_grad.astype(BF)
    grad_a = jnp.concatenate([(product_grad * x_part[:rows]).astype(BF), c_grad[:, :quarter]], axis=1)
    grad_b = jnp.concatenate([c_grad[:, quarter:], (product_grad * b_part[:rows]).astype(BF)], axis=1)
    gate_pass = scatter_pass(gate_far)
    up_pass = scatter_pass(up_far)
    down_pass = scatter_pass(down_far_terms)
    gate_sum = scatter_near(*gate_far, gate_pass, "z").astype(BF)
    up_sum = scatter_near(*up_far, up_pass, "x").astype(BF)
    down_sum = scatter_near(*down_far_terms, down_pass, "y").astype(BF)
    down_sum = jnp.where(core == 0, down_sum, down_sum[::-1])
    down_sum = down_sum.reshape(4, 4, ff // 64, half)
    normed_part = contract(grad_a, in_a, 1, 1) + contract(grad_b, in_b, 1, 1)
    gain_one_grad = jnp.sum(normed_part * scaled_one[:rows], axis=0)
    tap_full = lax.dynamic_update_slice(
        jnp.zeros((3, d_model), F32), tap_grads, (0, core * half)
    )
    extra = jnp.concatenate(
        [gain_one_grad[None], tap_full, gain_two_grad[None], jnp.zeros((123, d_model), F32)]
    ).astype(BF)
    left_b = after(normed[:rows], grad_b, up_pass)
    left_a = after(normed[:rows], gate_pass)
    left_c = after(gated_full[:rows], grad_b, down_pass)
    far_b = scatter_dot(orders["x"], left_b, grad_b, "x")
    far_a = scatter_dot(orders["z"], left_a, grad_a, "z", extra)
    far_c = scatter_dot(orders["y"], left_c, out_right, "y")
    far_a, far_b = ((after(far[0], down_pass, far_c[3]), *far[1:]) for far in (far_a, far_b))
    mix_b = scatter_near(*far_b, scatter_pass(far_b), "x").astype(BF)
    mix_a = scatter_near(*far_a, scatter_pass(far_a), "z").astype(BF)
    mix_c = scatter_near(*far_c, scatter_pass(far_c), "y").astype(BF)

    got = swap_core(lax.dynamic_slice(normed_part, ((1 - core) * length, 0), (length, d_model)))
    normed_grad = lax.dynamic_slice(normed_part, own_at, (length, d_model)) + got
    tokens_grad = (
        lax.dynamic_slice(middle_grad, own_at, (length, d_model))
        + norm_backward(
            lax.dynamic_slice(scaled_one, own_at, (length, d_model)),
            lax.dynamic_slice(inverse_one, own_at, (length, 1)),
            gain_first,
            normed_grad,
        )
    ).astype(BF)

    flow_a = jnp.concatenate([mix_a, gate_sum], axis=-1)
    flow_b = jnp.concatenate([mix_b, up_sum], axis=-1)
    flow_c = jnp.concatenate([mix_c, down_sum], axis=-2)
    trades = [("x", 0), ("y", 0), ("z", 1)]
    fars = [scatter_far(place, f, *at) for f, at in zip((flow_a, flow_b, flow_c), trades)]
    passes = [scatter_pass(far) for far in fars]
    flow_a, flow_b, flow_c = (
        after(scatter_near(*far, passing, at[0]).astype(BF), *passes)
        for far, passing, at in zip(fars, passes, trades)
    )
    flow_a = scatter_small(place, flow_a, "y")
    flow_b = scatter_small(place, flow_b, "z")
    flow_c = scatter_small(place, flow_c, "x")

    lead = own_rows // 2
    deep = (flow_c.shape[0] - own_rows) // 2

    def other_rows(flow, first, count):
        return swap_core(
            jnp.where(core == 0, flow[first + count : first + 2 * count], flow[first : first + count])
        )

    got = [
        other_rows(flow_a, 0, lead),
        other_rows(flow_b, 0, lead),
        other_rows(flow_c, 0, lead),
        other_rows(flow_c, own_rows, deep),
    ]
    in_grad, gate_grad, up_grad, out_grad, down_grad, norm_grad, tap_grad, ffn_norm_grad = finish(
        core, [flow_a, flow_b, flow_c, *got], half, ff_half
    )
    return (
        block_output,
        tokens_grad,
        norm_grad,
        in_grad,
        tap_grad,
        out_grad,
        ffn_norm_grad,
        gate_grad,
        up_grad,
        down_grad,
    )


def solution(mesh):
    return jax.shard_map(
        on_device,
        mesh=mesh,
        in_specs=(
            P("fsdp", None),
            P("fsdp"),
            P("fsdp", None),
            P(None, "fsdp"),
            P("fsdp", None),
            P("fsdp"),
            P("fsdp", None),
            P("fsdp", None),
            P("fsdp", None),
            P(),
            P("fsdp", None),
        ),
        out_specs=(
            P("fsdp", None),
            P("fsdp", None),
            P("fsdp"),
            P("fsdp", None),
            P(None, "fsdp"),
            P("fsdp", None),
            P("fsdp"),
            P("fsdp", None),
            P("fsdp", None),
            P("fsdp", None),
        ),
        check_vma=False,
    )
```

```python
import jax
import jax.numpy as jnp
from jax import lax
from jax.experimental import pallas as pl
from jax.experimental.pallas import tpu as pltpu
from jax.sharding import PartitionSpec as P

EPS = 1e-05
AXES = {"x": 5, "y": 3, "z": 1}
DIM = {"x": 0, "y": 1, "z": 2}
BF = jnp.bfloat16
F32 = jnp.float32


def contract(left, right, left_dim, right_dim):
    return lax.dot_general(
        left, right, (((left_dim,), (right_dim,)), ((), ())), preferred_element_type=F32
    )


def swap_core(value):
    return lax.ppermute(value, "fsdp", [(d, d ^ 1) for d in range(128)])


def swap_chip(value, axis, masks):
    low = AXES[axis]
    return lax.ppermute(value, "fsdp", [(d, d ^ (masks[d & 1] << low)) for d in range(128)])


def next_chip(value, by):
    return lax.ppermute(
        value, "fsdp", [(d, d + 2 * by) for d in range(128) if 0 <= d + 2 * by < 128]
    )


class Place:
    def __init__(self):
        device = lax.axis_index("fsdp")
        self.device = device
        self.core = device & 1
        self.chip = device >> 1
        self.at = {axis: (device >> low) & 3 for axis, low in AXES.items()}


def by_core(core, mine, other, axis):
    first = jnp.where(core == 0, mine, other)
    second = jnp.where(core == 0, other, mine)
    return jnp.concatenate([first, second], axis=axis)


def after(value, *before):
    return lax.optimization_barrier((value, *before))[0]


def arrange(core, pairs, half, ff_half):
    quarter = half // 2
    rows = 2 * pairs[0].shape[0]
    deep = 2 * pairs[8].shape[0]

    def kernel(core_ref, *refs):
        ins, (flow_a, flow_b, flow_c) = refs[:10], refs[10:]

        def columns(which, start, width, step):
            mine, other = ins[2 * which], ins[2 * which + 1]
            zero = [mine[:, start : start + width], other[:, start : start + width]]
            start += step
            one = [other[:, start : start + width], mine[:, start : start + width]]
            picked = [
                jnp.where(core_ref[0] == 0, z.astype(F32), o.astype(F32)) for z, o in zip(zero, one)
            ]
            return jnp.concatenate(picked, axis=0)

        def upright(zero, one):
            zero, one = zero[:, 2 * half :].astype(F32), one[:, 2 * half :].astype(F32)
            vectors = jnp.where(core_ref[0] == 0, zero, one)
            square = jnp.concatenate([vectors, jnp.zeros((120, 128), F32)], axis=0)
            return square.T[:8]

        flow_a[:, :half] = columns(0, 0, half, half).astype(BF)
        flow_a[:, half : half + quarter] = columns(0, 2 * half, quarter, half).astype(BF)
        flow_a[:, half + quarter : half + quarter + 128] = jnp.concatenate(
            [upright(ins[6], ins[7]), upright(ins[7], ins[6])], axis=0
        ).astype(BF)
        flow_a[:, half + quarter + 128 :] = columns(1, 0, ff_half, ff_half).astype(BF)
        flow_b[:, :quarter] = columns(0, 2 * half + quarter, quarter, half).astype(BF)
        flow_b[:, quarter : quarter + half] = columns(0, 4 * half, half, half).astype(BF)
        flow_b[:, half + quarter :] = columns(2, 0, ff_half, ff_half).astype(BF)
        last = [columns(3, 0, half, half), columns(4, 0, half, half)]
        flow_c[...] = jnp.concatenate(last, axis=0).astype(BF)

    vmem = pl.BlockSpec(memory_space=pltpu.VMEM)
    wide_a = jax.ShapeDtypeStruct((rows, half + quarter + 128 + ff_half), BF)
    wide_b = jax.ShapeDtypeStruct((rows, half + quarter + ff_half), BF)
    return pl.pallas_call(
        kernel,
        out_shape=[wide_a, wide_b, jax.ShapeDtypeStruct((rows + deep, half), BF)],
        in_specs=[pl.BlockSpec(memory_space=pltpu.SMEM)] + [vmem] * 10,
        out_specs=[vmem] * 3,
        name="arrange",
    )(core.reshape(1), *pairs)


def finish(core, arrays, half, ff_half):
    quarter = half // 2
    side = half + quarter
    few = arrays[3].shape[0]
    deep = arrays[6].shape[0]

    def kernel(core_ref, *refs):
        flow_a, flow_b, flow_c, got_a, got_b, got_out, got_down = refs[:7]
        in_grad, gate_grad, up_grad, out_grad, down_grad, norm_grad, tap_grad, ffn_norm_grad = refs[7:]
        first = core_ref[0] == 0

        def own(flow, start, count, lanes):
            return jnp.where(
                first, flow[start : start + count, lanes], flow[start + count : start + 2 * count, lanes]
            )

        def both(ref, at, mine, other):
            width = mine.shape[1]
            ref[:, at : at + width] = jnp.where(first, mine, other)
            at += ref.shape[1] // 2 if ref is not in_grad else half
            ref[:, at : at + width] = jnp.where(first, other, mine)

        def rows(flow, got, at, lanes, ref):
            both(ref, at, own(flow, 0, few, lanes), got[:, lanes])

        rows(flow_a, got_a, 0, slice(0, half), in_grad)
        rows(flow_a, got_a, 2 * half, slice(half, side), in_grad)
        rows(flow_b, got_b, 2 * half + quarter, slice(0, quarter), in_grad)
        rows(flow_b, got_b, 4 * half, slice(quarter, side), in_grad)
        rows(flow_a, got_a, 0, slice(side + 128, side + 128 + ff_half), gate_grad)
        rows(flow_b, got_b, 0, slice(side, side + ff_half), up_grad)
        rows(flow_c, got_out, 0, slice(0, half), out_grad)
        both(down_grad, 0, own(flow_c, 2 * few, deep, slice(0, half)), got_down[...])
        lanes = slice(side, side + 128)
        vectors = own(flow_a, 0, few, lanes) + got_a[:, lanes]
        square = jnp.concatenate([vectors, jnp.zeros((128 - few, 128), F32)], axis=0)
        square = square.T[:, :few]
        norm_grad[...] = square[0]
        tap_grad[...] = square[1:4]
        ffn_norm_grad[...] = square[4]

    vmem = pl.BlockSpec(memory_space=pltpu.VMEM)
    shapes = [(few, 6 * half), (few, 2 * ff_half), (few, 2 * ff_half), (few, 2 * half), (deep, 2 * half)]
    shapes += [(few,), (3, few), (few,)]
    return pl.pallas_call(
        kernel,
        out_shape=[jax.ShapeDtypeStruct(shape, F32) for shape in shapes],
        in_specs=[pl.BlockSpec(memory_space=pltpu.SMEM)] + [vmem] * 7,
        out_specs=[vmem] * 8,
        name="finish",
    )(core.reshape(1), *arrays)


def put(place, parts, axis, dim):
    block = parts[0][1]
    me = place.at[axis]
    shape = block.shape[:dim] + (4,) + block.shape[dim:]
    out = jnp.zeros(shape, block.dtype)
    for code, part in parts:
        where = [jnp.int32(0)] * len(shape)
        where[dim] = me ^ code
        out = lax.dynamic_update_slice(out, jnp.expand_dims(part, dim), where)
    return out


def gather_far(place, block, near, axis, dim):
    sent = jnp.stack([block, near])
    far = swap_chip(sent, axis, (3, 1))
    one = jnp.where(place.core == 0, 1, 3)
    return put(place, ((0, block), (one, near), (4 - one, far[0]), (2, far[1])), axis, dim), sent


def gather_axis(place, block, axis, dim):
    return gather_far(place, block, swap_chip(block, axis, (1, 3)), axis, dim)[0]


def scatter_far(place, terms, axis, dim):
    me = place.at[axis]
    one = jnp.where(place.core == 0, 3, 1)

    def take(code):
        if isinstance(terms, list):
            return jnp.stack(
                [lax.dynamic_index_in_dim(t, me ^ code, dim, keepdims=False) for t in terms]
            )
        return lax.dynamic_index_in_dim(terms, me ^ code, dim, keepdims=False)

    sent = jnp.stack([take(one), take(2)])
    return swap_chip(sent, axis, (3, 1)), take(4 - one), take(jnp.int32(0)), sent


def block_order(place, axis):
    spot = jnp.arange(1024, dtype=jnp.int32)
    one = jnp.where(place.core == 0, 1, 3)
    which = spot >> 8
    code = jnp.where(which == 0, 0, jnp.where(which == 1, one, jnp.where(which == 2, 4 - one, 2)))
    there = place.at[axis] ^ code
    high, low, inner = (spot >> 6) & 3, (spot >> 4) & 3, spot & 15
    x, y, z = {"x": (there, high, low), "y": (high, there, low), "z": (high, low, there)}[axis]
    source = x * 256 + y * 64 + z * 16 + inner
    return (source[:, None] == spot[None, :]).astype(BF)


def scatter_dot(order, left, right, axis, extra=None):
    left = contract(order, left, 1, 1).astype(BF)
    if extra is not None:
        extra = contract(order, extra, 1, 1).astype(BF)

    def terms(part):
        product = jnp.dot(left[part], right, preferred_element_type=F32).astype(BF)
        if extra is not None:
            product = jnp.concatenate([product, extra[part]], axis=1)
        return product.reshape(2, 4, 4, 16, product.shape[-1])

    sent = terms(slice(512, None))
    keep = terms(slice(None, 512))
    return swap_chip(sent, axis, (3, 1)), keep[1], keep[0], sent


def scatter_pass(half_way):
    far, passing = half_way[:2]
    return (passing.astype(F32) + far[1].astype(F32)).astype(BF)


def scatter_near(far, _, own, __, passing, axis):
    near = swap_chip(passing, axis, (1, 3))
    return own.astype(F32) + far[0].astype(F32) + near.astype(F32)


def scatter_axis(place, terms, axis, dim):
    half_way = scatter_far(place, terms, axis, dim)
    return scatter_near(*half_way, scatter_pass(half_way), axis)


def scatter_small(place, terms, axis):
    total = 0.0
    for code in (1, 3, 2):
        there = lax.dynamic_index_in_dim(terms, place.at[axis] ^ code, 0, keepdims=False)
        total = total + swap_chip(there, axis, (code, code)).astype(F32)
    own = lax.dynamic_index_in_dim(terms, place.at[axis], 0, keepdims=False)
    return total + own.astype(F32)


def inverse_rms(values):
    return lax.rsqrt(jnp.mean(values * values, axis=-1, keepdims=True) + EPS)


def norm_backward(scaled, inverse, gain, upstream):
    inner = upstream * gain
    return inverse * (inner - scaled * jnp.mean(inner * scaled, axis=-1, keepdims=True))


def halves(array):
    mid = array.shape[-1] // 2
    return (array[..., :mid], array[..., mid:])


def on_device(
    tokens,
    norm_gain,
    in_weight,
    conv_weight,
    out_weight,
    ffn_gain,
    gate_weight,
    up_weight,
    down_weight,
    seq_start,
    out_grad,
):
    place = Place()
    core = place.core
    length = tokens.shape[0]
    rows = 2 * length
    d_model = tokens.shape[1]
    half = d_model // 2
    quarter = half // 2
    ff = gate_weight.shape[1]
    ff_half = ff // 2
    side = 3 * quarter

    kinds = jnp.concatenate([norm_gain[None], conv_weight, ffn_gain[None]])
    kinds = jnp.pad(kinds, ((0, 3), (0, 120)))
    shards = [in_weight, gate_weight, up_weight, jnp.concatenate([out_weight, kinds], 1), down_weight]
    pairs = [array for shard in shards for array in (shard, swap_core(shard))]
    full = rows + 8
    cut_a = side + 128 + ff_half
    cut_b = cut_a + side + ff_half
    flow_a, flow_b, flow_c = arrange(core, pairs, half, ff_half)
    own_rows = 2 * norm_gain.shape[0]

    flow_a = gather_axis(place, flow_a, "x", 0)
    flow_b = gather_axis(place, flow_b, "y", 0)
    flow_c = gather_axis(place, flow_c, "z", 0)
    tokens, out_grad = after((tokens, out_grad), flow_a, flow_b, flow_c)
    both = jnp.stack([tokens, out_grad])
    both = by_core(core, both, swap_core(both), 1)
    flow_a = gather_axis(place, flow_a, "y", 1)
    flow_b = gather_axis(place, flow_b, "z", 1)
    flow_c = gather_axis(place, flow_c, "x", 0)
    near_a = swap_chip(flow_a, "z", (1, 3))
    near_b = swap_chip(flow_b, "x", (1, 3))
    near_c = swap_chip(flow_c, "y", (1, 3))
    mix_cut = side + 128

    edges = after((both[:, :2], both[0, rows - 2 :]), flow_a, flow_b, flow_c)
    from_next = next_chip(edges[0], -1)
    from_last = next_chip(edges[1], 1)
    mix_a, sent_a = gather_far(place, flow_a[..., :mix_cut], near_a[..., :mix_cut], "z", 2)
    mix_b, sent_b = gather_far(place, flow_b[..., :side], near_b[..., :side], "x", 0)
    mix_c, sent_c = gather_far(
        place, flow_c[:, :, :own_rows], near_c[:, :, :own_rows], "y", 1
    )
    from_next, from_last = after((from_next, from_last), sent_a, sent_b, sent_c)
    spare = jnp.zeros((4, d_model), BF)
    tok = jnp.concatenate([both[0], from_next[0], from_last, spare])
    grad_out = jnp.concatenate([both[1], from_next[1], from_last * 0, spare])
    flow_a, near_a = after((flow_a[..., mix_cut:], near_a[..., mix_cut:]), sent_a)
    flow_b, near_b = after((flow_b[..., side:], near_b[..., side:]), sent_b)
    flow_c, near_c = after((flow_c[:, :, own_rows:], near_c[:, :, own_rows:]), sent_c)
    gate_c, sent_a = gather_far(place, flow_a, near_a, "z", 2)
    up_c, sent_b = gather_far(place, flow_b, near_b, "x", 0)
    down_cols, sent_c = gather_far(place, flow_c, near_c, "y", 1)
    gate_c, up_c = gate_c.reshape(d_model, ff_half), up_c.reshape(d_model, ff_half)
    down_cols = down_cols.reshape(ff, half)
    mix_a = mix_a.reshape(d_model, mix_cut)
    mix_b = mix_b.reshape(d_model, side)
    mix_c = mix_c.reshape(d_model, half)

    in_a, in_b = mix_a[:, :side], mix_b
    smalls = mix_a[:, side:].T[:8].astype(F32)
    gain_first, gain_second = smalls[0], smalls[4]
    taps = lax.dynamic_slice(smalls, (1, core * half), (3, half))
    out_full = by_core(core, mix_c, swap_core(mix_c), 1)

    blocks = jnp.arange(seq_start.shape[0], dtype=jnp.int32)
    starts = jnp.where(seq_start < length, blocks * length + seq_start, -9)[None, :]
    places = 2 * length * place.chip + jnp.arange(full, dtype=jnp.int32)[:, None]
    begins_here = jnp.any(starts == places, axis=1, keepdims=True)
    begins_before = jnp.any(starts == places - 1, axis=1, keepdims=True)
    lag_one = jnp.where(begins_here, 0.0, 1.0).astype(F32)
    lag_two = jnp.where(begins_here | begins_before, 0.0, 1.0).astype(F32)

    hidden = tok.astype(F32)
    inverse_one = inverse_rms(hidden)
    scaled_one = hidden * inverse_one
    normed = (scaled_one * gain_first).astype(BF)
    normed = after(normed, sent_a, sent_b, sent_c)
    proj_a = jnp.dot(normed, in_a, preferred_element_type=F32)
    proj_b = jnp.dot(normed, in_b, preferred_element_type=F32)
    b_part, x_part = proj_a[:, :half], proj_b[:, quarter:]
    c_part = jnp.concatenate([proj_a[:, half:], proj_b[:, :quarter]], axis=1)
    wide_product = lax.reduce_precision(b_part * x_part, exponent_bits=8, mantissa_bits=7)
    pad = wide_product[rows + 4 :]
    lagged_one = lag_one * jnp.concatenate(
        [wide_product[rows + 3 : rows + 4], wide_product[: rows + 1], pad, pad[:2]]
    )
    lagged_two = lag_two * jnp.concatenate(
        [wide_product[rows + 2 : rows + 4], wide_product[:rows], pad, pad[:2]]
    )
    convolved = taps[0] * wide_product + taps[1] * lagged_one + taps[2] * lagged_two
    gated = (c_part * convolved).astype(BF)
    gated_full = by_core(core, gated, swap_core(gated), 1)
    middle = hidden + jnp.dot(gated_full, out_full, preferred_element_type=F32)

    inverse_two = inverse_rms(middle)
    scaled_two = middle * inverse_two
    second = (scaled_two * gain_second).astype(BF)
    gate_value = jnp.dot(second, gate_c, preferred_element_type=F32)
    up_value = jnp.dot(second, up_c, preferred_element_type=F32)
    gate_sigmoid = jax.nn.sigmoid(gate_value)
    gate_silu = gate_value * gate_sigmoid
    activated = (gate_silu * up_value).astype(BF)
    grad_own = lax.dynamic_slice(grad_out, (0, core * half), (full, half))
    grad_far = lax.dynamic_slice(grad_out, (0, (1 - core) * half), (full, half))
    activated_far = swap_core(activated[:rows])
    down_own = lax.dynamic_slice(down_cols, (core * ff_half, 0), (ff_half, half))
    down_far = swap_core(lax.dynamic_slice(down_cols, ((1 - core) * ff_half, 0), (ff_half, half)))
    act_grad = contract(grad_own, down_own, 1, 1) + contract(grad_far, down_far, 1, 1)
    gate_grad = (
        act_grad * up_value * gate_sigmoid * (1.0 + gate_value * (1.0 - gate_sigmoid))
    ).astype(BF)
    up_grad = (act_grad * gate_silu).astype(BF)
    down_terms = [
        contract(part, grad_own[:rows], 0, 0).astype(BF).reshape(2, 4, 4, ff // 64, half)
        for part in (activated[:rows], activated_far)
    ]
    down_far_terms = scatter_far(place, down_terms, "y", 1)
    orders = {axis: block_order(place, axis) for axis in AXES}
    gate_far = scatter_dot(orders["z"], after(second[:rows], gate_grad), gate_grad[:rows], "z")
    up_far = scatter_dot(orders["x"], after(second[:rows], up_grad), up_grad[:rows], "x")
    gate_grad, up_grad = after((gate_grad, up_grad), gate_far[3], up_far[3], down_far_terms[3])
    second_part = contract(gate_grad, gate_c, 1, 1) + contract(up_grad, up_c, 1, 1)
    second_grad = second_part + swap_core(second_part)

    own_at = (core * length, 0)
    activated = after(activated[:rows], second_part)
    out_own = jnp.dot(activated, down_own, preferred_element_type=F32)
    out_far = jnp.dot(activated, down_far, preferred_element_type=F32)
    out_part = by_core(core, out_own, out_far, 1)
    got = swap_core(lax.dynamic_slice(out_part, ((1 - core) * length, 0), (length, d_model)))
    block_output = (
        lax.dynamic_slice(middle, own_at, (length, d_model))
        + lax.dynamic_slice(out_part, own_at, (length, d_model))
        + got
    ).astype(BF)

    middle_grad = grad_out.astype(F32) + norm_backward(
        scaled_two, inverse_two, gain_second, second_grad
    )
    gain_two_grad = jnp.sum((second_grad * scaled_two)[:rows], axis=0) * (core == 0).astype(F32)
    branch_grad = middle_grad.astype(BF)
    out_rows = lax.dynamic_slice(out_full, (core * half, 0), (half, d_model))
    gated_grad = contract(branch_grad, out_rows, 1, 1)
    out_right = lax.dynamic_slice(branch_grad, (0, core * half), (rows, half))
    convolved_grad = gated_grad * c_part
    c_grad = gated_grad * convolved
    from_one = taps[1] * lag_one * convolved_grad
    from_two = taps[2] * lag_two * convolved_grad
    convolved_grad, c_grad = convolved_grad[:rows], c_grad[:rows]
    product_grad = taps[0] * convolved_grad + from_one[1 : rows + 1] + from_two[2 : rows + 2]
    tap_grads = jnp.stack(
        [
            jnp.sum(convolved_grad * wide_product[:rows], axis=0),
            jnp.sum(convolved_grad * lagged_one[:rows], axis=0),
            jnp.sum(convolved_grad * lagged_two[:rows], axis=0),
        ]
    )
    c_grad = c_grad.astype(BF)
    grad_a = jnp.concatenate([(product_grad * x_part[:rows]).astype(BF), c_grad[:, :quarter]], axis=1)
    grad_b = jnp.concatenate([c_grad[:, quarter:], (product_grad * b_part[:rows]).astype(BF)], axis=1)
    gate_pass = scatter_pass(gate_far)
    up_pass = scatter_pass(up_far)
    down_pass = scatter_pass(down_far_terms)
    gate_sum = scatter_near(*gate_far, gate_pass, "z").astype(BF)
    up_sum = scatter_near(*up_far, up_pass, "x").astype(BF)
    down_sum = scatter_near(*down_far_terms, down_pass, "y").astype(BF)
    down_sum = jnp.where(core == 0, down_sum, down_sum[::-1])
    down_sum = down_sum.reshape(4, 4, ff // 64, half)
    normed_part = contract(grad_a, in_a, 1, 1) + contract(grad_b, in_b, 1, 1)
    gain_one_grad = jnp.sum(normed_part * scaled_one[:rows], axis=0)
    tap_full = lax.dynamic_update_slice(
        jnp.zeros((3, d_model), F32), tap_grads, (0, core * half)
    )
    extra = jnp.concatenate(
        [gain_one_grad[None], tap_full, gain_two_grad[None], jnp.zeros((123, d_model), F32)]
    ).astype(BF)
    left_b = after(normed[:rows], grad_b, up_pass)
    left_a = after(normed[:rows], gate_pass)
    left_c = after(gated_full[:rows], grad_b, down_pass)
    far_b = scatter_dot(orders["x"], left_b, grad_b, "x")
    far_a = scatter_dot(orders["z"], left_a, grad_a, "z", extra)
    far_c = scatter_dot(orders["y"], left_c, out_right, "y")
    far_a, far_b = ((after(far[0], down_pass, far_c[3]), *far[1:]) for far in (far_a, far_b))
    mix_b = scatter_near(*far_b, scatter_pass(far_b), "x").astype(BF)
    mix_a = scatter_near(*far_a, scatter_pass(far_a), "z").astype(BF)
    mix_c = scatter_near(*far_c, scatter_pass(far_c), "y").astype(BF)

    got = swap_core(lax.dynamic_slice(normed_part, ((1 - core) * length, 0), (length, d_model)))
    normed_grad = lax.dynamic_slice(normed_part, own_at, (length, d_model)) + got
    tokens_grad = (
        lax.dynamic_slice(middle_grad, own_at, (length, d_model))
        + norm_backward(
            lax.dynamic_slice(scaled_one, own_at, (length, d_model)),
            lax.dynamic_slice(inverse_one, own_at, (length, 1)),
            gain_first,
            normed_grad,
        )
    ).astype(BF)

    flow_a = jnp.concatenate([mix_a, gate_sum], axis=-1)
    flow_b = jnp.concatenate([mix_b, up_sum], axis=-1)
    flow_c = jnp.concatenate([mix_c, down_sum], axis=-2)
    trades = [("x", 0), ("y", 0), ("z", 1)]
    fars = [scatter_far(place, f, *at) for f, at in zip((flow_a, flow_b, flow_c), trades)]
    passes = [scatter_pass(far) for far in fars]
    flow_a, flow_b, flow_c = (
        after(scatter_near(*far, passing, at[0]).astype(BF), *passes)
        for far, passing, at in zip(fars, passes, trades)
    )
    flow_a = scatter_small(place, flow_a, "y")
    flow_b = scatter_small(place, flow_b, "z")
    flow_c = scatter_small(place, flow_c, "x")

    lead = own_rows // 2
    deep = (flow_c.shape[0] - own_rows) // 2

    def other_rows(flow, first, count):
        return swap_core(
            jnp.where(core == 0, flow[first + count : first + 2 * count], flow[first : first + count])
        )

    got = [
        other_rows(flow_a, 0, lead),
        other_rows(flow_b, 0, lead),
        other_rows(flow_c, 0, lead),
        other_rows(flow_c, own_rows, deep),
    ]
    in_grad, gate_grad, up_grad, out_grad, down_grad, norm_grad, tap_grad, ffn_norm_grad = finish(
        core, [flow_a, flow_b, flow_c, *got], half, ff_half
    )
    return (
        block_output,
        tokens_grad,
        norm_grad,
        in_grad,
        tap_grad,
        out_grad,
        ffn_norm_grad,
        gate_grad,
        up_grad,
        down_grad,
    )


def solution(mesh):
    return jax.shard_map(
        on_device,
        mesh=mesh,
        in_specs=(
            P("fsdp", None),
            P("fsdp"),
            P("fsdp", None),
            P(None, "fsdp"),
            P("fsdp", None),
            P("fsdp"),
            P("fsdp", None),
            P("fsdp", None),
            P("fsdp", None),
            P(),
            P("fsdp", None),
        ),
        out_specs=(
            P("fsdp", None),
            P("fsdp", None),
            P("fsdp"),
            P("fsdp", None),
            P(None, "fsdp"),
            P("fsdp", None),
            P("fsdp"),
            P("fsdp", None),
            P("fsdp", None),
            P("fsdp", None),
        ),
        check_vma=False,
    )
```

```python
import jax
import jax.numpy as jnp
from jax import lax
from jax.experimental import pallas as pl
from jax.experimental.pallas import tpu as pltpu
from jax.sharding import PartitionSpec as P

EPS = 1e-05
AXES = {"x": 5, "y": 3, "z": 1}
DIM = {"x": 0, "y": 1, "z": 2}
BF = jnp.bfloat16
F32 = jnp.float32


def contract(left, right, left_dim, right_dim):
    return lax.dot_general(
        left, right, (((left_dim,), (right_dim,)), ((), ())), preferred_element_type=F32
    )


def swap_core(value):
    return lax.ppermute(value, "fsdp", [(d, d ^ 1) for d in range(128)])


def swap_chip(value, axis, masks):
    low = AXES[axis]
    return lax.ppermute(value, "fsdp", [(d, d ^ (masks[d & 1] << low)) for d in range(128)])


def next_chip(value, by):
    return lax.ppermute(
        value, "fsdp", [(d, d + 2 * by) for d in range(128) if 0 <= d + 2 * by < 128]
    )


class Place:
    def __init__(self):
        device = lax.axis_index("fsdp")
        self.device = device
        self.core = device & 1
        self.chip = device >> 1
        self.at = {axis: (device >> low) & 3 for axis, low in AXES.items()}


def by_core(core, mine, other, axis):
    first = jnp.where(core == 0, mine, other)
    second = jnp.where(core == 0, other, mine)
    return jnp.concatenate([first, second], axis=axis)


def after(value, *before):
    return lax.optimization_barrier((value, *before))[0]


def arrange(core, pairs, half, ff_half):
    quarter = half // 2
    rows = 2 * pairs[0].shape[0]
    deep = 2 * pairs[8].shape[0]

    def kernel(core_ref, *refs):
        ins, (flow_a, flow_b, flow_c) = refs[:10], refs[10:]

        def columns(which, start, width, step):
            mine, other = ins[2 * which], ins[2 * which + 1]
            zero = [mine[:, start : start + width], other[:, start : start + width]]
            start += step
            one = [other[:, start : start + width], mine[:, start : start + width]]
            picked = [
                jnp.where(core_ref[0] == 0, z.astype(F32), o.astype(F32)) for z, o in zip(zero, one)
            ]
            return jnp.concatenate(picked, axis=0)

        def upright(zero, one):
            zero, one = zero[:, 2 * half :].astype(F32), one[:, 2 * half :].astype(F32)
            vectors = jnp.where(core_ref[0] == 0, zero, one)
            square = jnp.concatenate([vectors, jnp.zeros((120, 128), F32)], axis=0)
            return square.T[:8]

        flow_a[:, :half] = columns(0, 0, half, half).astype(BF)
        flow_a[:, half : half + quarter] = columns(0, 2 * half, quarter, half).astype(BF)
        flow_a[:, half + quarter : half + quarter + 128] = jnp.concatenate(
            [upright(ins[6], ins[7]), upright(ins[7], ins[6])], axis=0
        ).astype(BF)
        flow_a[:, half + quarter + 128 :] = columns(1, 0, ff_half, ff_half).astype(BF)
        flow_b[:, :quarter] = columns(0, 2 * half + quarter, quarter, half).astype(BF)
        flow_b[:, quarter : quarter + half] = columns(0, 4 * half, half, half).astype(BF)
        flow_b[:, half + quarter :] = columns(2, 0, ff_half, ff_half).astype(BF)
        last = [columns(3, 0, half, half), columns(4, 0, half, half)]
        flow_c[...] = jnp.concatenate(last, axis=0).astype(BF)

    vmem = pl.BlockSpec(memory_space=pltpu.VMEM)
    wide_a = jax.ShapeDtypeStruct((rows, half + quarter + 128 + ff_half), BF)
    wide_b = jax.ShapeDtypeStruct((rows, half + quarter + ff_half), BF)
    return pl.pallas_call(
        kernel,
        out_shape=[wide_a, wide_b, jax.ShapeDtypeStruct((rows + deep, half), BF)],
        in_specs=[pl.BlockSpec(memory_space=pltpu.SMEM)] + [vmem] * 10,
        out_specs=[vmem] * 3,
        name="arrange",
    )(core.reshape(1), *pairs)


def finish(core, arrays, half, ff_half):
    quarter = half // 2
    side = half + quarter
    few = arrays[3].shape[0]
    deep = arrays[6].shape[0]

    def kernel(core_ref, *refs):
        flow_a, flow_b, flow_c, got_a, got_b, got_out, got_down = refs[:7]
        in_grad, gate_grad, up_grad, out_grad, down_grad, norm_grad, tap_grad, ffn_norm_grad = refs[7:]
        first = core_ref[0] == 0

        def own(flow, start, count, lanes):
            return jnp.where(
                first, flow[start : start + count, lanes], flow[start + count : start + 2 * count, lanes]
            )

        def both(ref, at, mine, other):
            width = mine.shape[1]
            ref[:, at : at + width] = jnp.where(first, mine, other)
            at += ref.shape[1] // 2 if ref is not in_grad else half
            ref[:, at : at + width] = jnp.where(first, other, mine)

        def rows(flow, got, at, lanes, ref):
            both(ref, at, own(flow, 0, few, lanes), got[:, lanes])

        rows(flow_a, got_a, 0, slice(0, half), in_grad)
        rows(flow_a, got_a, 2 * half, slice(half, side), in_grad)
        rows(flow_b, got_b, 2 * half + quarter, slice(0, quarter), in_grad)
        rows(flow_b, got_b, 4 * half, slice(quarter, side), in_grad)
        rows(flow_a, got_a, 0, slice(side + 128, side + 128 + ff_half), gate_grad)
        rows(flow_b, got_b, 0, slice(side, side + ff_half), up_grad)
        rows(flow_c, got_out, 0, slice(0, half), out_grad)
        both(down_grad, 0, own(flow_c, 2 * few, deep, slice(0, half)), got_down[...])
        lanes = slice(side, side + 128)
        vectors = own(flow_a, 0, few, lanes) + got_a[:, lanes]
        square = jnp.concatenate([vectors, jnp.zeros((128 - few, 128), F32)], axis=0)
        square = square.T[:, :few]
        norm_grad[...] = square[0]
        tap_grad[...] = square[1:4]
        ffn_norm_grad[...] = square[4]

    vmem = pl.BlockSpec(memory_space=pltpu.VMEM)
    shapes = [(few, 6 * half), (few, 2 * ff_half), (few, 2 * ff_half), (few, 2 * half), (deep, 2 * half)]
    shapes += [(few,), (3, few), (few,)]
    return pl.pallas_call(
        kernel,
        out_shape=[jax.ShapeDtypeStruct(shape, F32) for shape in shapes],
        in_specs=[pl.BlockSpec(memory_space=pltpu.SMEM)] + [vmem] * 7,
        out_specs=[vmem] * 8,
        name="finish",
    )(core.reshape(1), *arrays)


def put(place, parts, axis, dim):
    block = parts[0][1]
    me = place.at[axis]
    shape = block.shape[:dim] + (4,) + block.shape[dim:]
    out = jnp.zeros(shape, block.dtype)
    for code, part in parts:
        where = [jnp.int32(0)] * len(shape)
        where[dim] = me ^ code
        out = lax.dynamic_update_slice(out, jnp.expand_dims(part, dim), where)
    return out


def gather_far(place, block, near, axis, dim):
    sent = jnp.stack([block, near])
    far = swap_chip(sent, axis, (3, 1))
    one = jnp.where(place.core == 0, 1, 3)
    return put(place, ((0, block), (one, near), (4 - one, far[0]), (2, far[1])), axis, dim), sent


def gather_axis(place, block, axis, dim):
    return gather_far(place, block, swap_chip(block, axis, (1, 3)), axis, dim)[0]


def scatter_far(place, terms, axis, dim):
    me = place.at[axis]
    one = jnp.where(place.core == 0, 3, 1)

    def take(code):
        if isinstance(terms, list):
            return jnp.stack(
                [lax.dynamic_index_in_dim(t, me ^ code, dim, keepdims=False) for t in terms]
            )
        return lax.dynamic_index_in_dim(terms, me ^ code, dim, keepdims=False)

    sent = jnp.stack([take(one), take(2)])
    return swap_chip(sent, axis, (3, 1)), take(4 - one), take(jnp.int32(0)), sent


def block_order(place, axis):
    spot = jnp.arange(1024, dtype=jnp.int32)
    one = jnp.where(place.core == 0, 1, 3)
    which = spot >> 8
    code = jnp.where(which == 0, 0, jnp.where(which == 1, one, jnp.where(which == 2, 4 - one, 2)))
    there = place.at[axis] ^ code
    high, low, inner = (spot >> 6) & 3, (spot >> 4) & 3, spot & 15
    x, y, z = {"x": (there, high, low), "y": (high, there, low), "z": (high, low, there)}[axis]
    source = x * 256 + y * 64 + z * 16 + inner
    return (source[:, None] == spot[None, :]).astype(BF)


def scatter_dot(order, left, right, axis, extra=None, late=False):
    left = contract(order, left, 1, 1).astype(BF)
    if extra is not None:
        extra = contract(order, extra, 1, 1).astype(BF)

    def terms(part):
        product = jnp.dot(left[part], right, preferred_element_type=F32).astype(BF)
        if extra is not None:
            product = jnp.concatenate([product, extra[part]], axis=1)
        return product.reshape(2, 4, 4, 16, product.shape[-1])

    sent = terms(slice(512, None))
    got = swap_chip(sent, axis, (3, 1))
    if late:
        return got, left[:512], None, sent
    keep = terms(slice(None, 512))
    return got, keep[1], keep[0], sent


def scatter_keep(half_way, right, before):
    product = jnp.dot(after(half_way[1], before), right, preferred_element_type=F32).astype(BF)
    keep = product.reshape(2, 4, 4, 16, right.shape[-1])
    return half_way[0], keep[1], keep[0], half_way[3]


def scatter_pass(half_way):
    far, passing = half_way[:2]
    return (passing.astype(F32) + far[1].astype(F32)).astype(BF)


def scatter_near(far, _, own, __, passing, axis):
    near = swap_chip(passing, axis, (1, 3))
    return own.astype(F32) + far[0].astype(F32) + near.astype(F32)


def scatter_axis(place, terms, axis, dim):
    half_way = scatter_far(place, terms, axis, dim)
    return scatter_near(*half_way, scatter_pass(half_way), axis)


def scatter_small(place, terms, axis):
    total = 0.0
    for code in (1, 3, 2):
        there = lax.dynamic_index_in_dim(terms, place.at[axis] ^ code, 0, keepdims=False)
        total = total + swap_chip(there, axis, (code, code)).astype(F32)
    own = lax.dynamic_index_in_dim(terms, place.at[axis], 0, keepdims=False)
    return total + own.astype(F32)


def inverse_rms(values):
    return lax.rsqrt(jnp.mean(values * values, axis=-1, keepdims=True) + EPS)


def norm_backward(scaled, inverse, gain, upstream):
    inner = upstream * gain
    return inverse * (inner - scaled * jnp.mean(inner * scaled, axis=-1, keepdims=True))


def halves(array):
    mid = array.shape[-1] // 2
    return (array[..., :mid], array[..., mid:])


def on_device(
    tokens,
    norm_gain,
    in_weight,
    conv_weight,
    out_weight,
    ffn_gain,
    gate_weight,
    up_weight,
    down_weight,
    seq_start,
    out_grad,
):
    place = Place()
    core = place.core
    length = tokens.shape[0]
    rows = 2 * length
    d_model = tokens.shape[1]
    half = d_model // 2
    quarter = half // 2
    ff = gate_weight.shape[1]
    ff_half = ff // 2
    side = 3 * quarter

    kinds = jnp.concatenate([norm_gain[None], conv_weight, ffn_gain[None]])
    kinds = jnp.pad(kinds, ((0, 3), (0, 120)))
    shards = [in_weight, gate_weight, up_weight, jnp.concatenate([out_weight, kinds], 1), down_weight]
    pairs = [array for shard in shards for array in (shard, swap_core(shard))]
    full = rows + 8
    cut_a = side + 128 + ff_half
    cut_b = cut_a + side + ff_half
    flow_a, flow_b, flow_c = arrange(core, pairs, half, ff_half)
    own_rows = 2 * norm_gain.shape[0]

    flow_a = gather_axis(place, flow_a, "x", 0)
    flow_b = gather_axis(place, flow_b, "y", 0)
    flow_c = gather_axis(place, flow_c, "z", 0)
    tokens, out_grad = after((tokens, out_grad), flow_a, flow_b, flow_c)
    both = jnp.stack([tokens, out_grad])
    both = by_core(core, both, swap_core(both), 1)
    flow_a = gather_axis(place, flow_a, "y", 1)
    flow_b = gather_axis(place, flow_b, "z", 1)
    flow_c = gather_axis(place, flow_c, "x", 0)
    near_a = swap_chip(flow_a, "z", (1, 3))
    near_b = swap_chip(flow_b, "x", (1, 3))
    near_c = swap_chip(flow_c, "y", (1, 3))
    mix_cut = side + 128

    edges = after((both[:, :2], both[0, rows - 2 :]), flow_a, flow_b, flow_c)
    from_next = next_chip(edges[0], -1)
    from_last = next_chip(edges[1], 1)
    mix_a, sent_a = gather_far(place, flow_a[..., :mix_cut], near_a[..., :mix_cut], "z", 2)
    mix_b, sent_b = gather_far(place, flow_b[..., :side], near_b[..., :side], "x", 0)
    mix_c, sent_c = gather_far(
        place, flow_c[:, :, :own_rows], near_c[:, :, :own_rows], "y", 1
    )
    from_next, from_last = after((from_next, from_last), sent_a, sent_b, sent_c)
    spare = jnp.zeros((4, d_model), BF)
    tok = jnp.concatenate([both[0], from_next[0], from_last, spare])
    grad_out = jnp.concatenate([both[1], from_next[1], from_last * 0, spare])
    flow_a, near_a = after((flow_a[..., mix_cut:], near_a[..., mix_cut:]), sent_a)
    flow_b, near_b = after((flow_b[..., side:], near_b[..., side:]), sent_b)
    flow_c, near_c = after((flow_c[:, :, own_rows:], near_c[:, :, own_rows:]), sent_c)
    gate_c, sent_a = gather_far(place, flow_a, near_a, "z", 2)
    up_c, sent_b = gather_far(place, flow_b, near_b, "x", 0)
    down_cols, sent_c = gather_far(place, flow_c, near_c, "y", 1)
    gate_c, up_c = gate_c.reshape(d_model, ff_half), up_c.reshape(d_model, ff_half)
    down_cols = down_cols.reshape(ff, half)
    mix_a = mix_a.reshape(d_model, mix_cut)
    mix_b = mix_b.reshape(d_model, side)
    mix_c = mix_c.reshape(d_model, half)

    in_a, in_b = mix_a[:, :side], mix_b
    smalls = mix_a[:, side:].T[:8].astype(F32)
    gain_first, gain_second = smalls[0], smalls[4]
    taps = lax.dynamic_slice(smalls, (1, core * half), (3, half))
    out_full = by_core(core, mix_c, swap_core(mix_c), 1)

    blocks = jnp.arange(seq_start.shape[0], dtype=jnp.int32)
    starts = jnp.where(seq_start < length, blocks * length + seq_start, -9)[None, :]
    places = 2 * length * place.chip + jnp.arange(full, dtype=jnp.int32)[:, None]
    begins_here = jnp.any(starts == places, axis=1, keepdims=True)
    begins_before = jnp.any(starts == places - 1, axis=1, keepdims=True)
    lag_one = jnp.where(begins_here, 0.0, 1.0).astype(F32)
    lag_two = jnp.where(begins_here | begins_before, 0.0, 1.0).astype(F32)

    hidden = tok.astype(F32)
    inverse_one = inverse_rms(hidden)
    scaled_one = hidden * inverse_one
    normed = (scaled_one * gain_first).astype(BF)
    normed = after(normed, sent_a, sent_b, sent_c)
    proj_a = jnp.dot(normed, in_a, preferred_element_type=F32)
    proj_b = jnp.dot(normed, in_b, preferred_element_type=F32)
    b_part, x_part = proj_a[:, :half], proj_b[:, quarter:]
    c_part = jnp.concatenate([proj_a[:, half:], proj_b[:, :quarter]], axis=1)
    wide_product = lax.reduce_precision(b_part * x_part, exponent_bits=8, mantissa_bits=7)
    pad = wide_product[rows + 4 :]
    lagged_one = lag_one * jnp.concatenate(
        [wide_product[rows + 3 : rows + 4], wide_product[: rows + 1], pad, pad[:2]]
    )
    lagged_two = lag_two * jnp.concatenate(
        [wide_product[rows + 2 : rows + 4], wide_product[:rows], pad, pad[:2]]
    )
    convolved = taps[0] * wide_product + taps[1] * lagged_one + taps[2] * lagged_two
    gated = (c_part * convolved).astype(BF)
    gated_full = by_core(core, gated, swap_core(gated), 1)
    middle = hidden + jnp.dot(gated_full, out_full, preferred_element_type=F32)

    inverse_two = inverse_rms(middle)
    scaled_two = middle * inverse_two
    second = (scaled_two * gain_second).astype(BF)
    gate_value = jnp.dot(second, gate_c, preferred_element_type=F32)
    up_value = jnp.dot(second, up_c, preferred_element_type=F32)
    gate_sigmoid = jax.nn.sigmoid(gate_value)
    gate_silu = gate_value * gate_sigmoid
    activated = (gate_silu * up_value).astype(BF)
    grad_own = lax.dynamic_slice(grad_out, (0, core * half), (full, half))
    grad_far = lax.dynamic_slice(grad_out, (0, (1 - core) * half), (full, half))
    activated_far = swap_core(activated[:rows])
    down_own = lax.dynamic_slice(down_cols, (core * ff_half, 0), (ff_half, half))
    down_far = swap_core(lax.dynamic_slice(down_cols, ((1 - core) * ff_half, 0), (ff_half, half)))
    act_grad = contract(grad_own, down_own, 1, 1) + contract(grad_far, down_far, 1, 1)
    gate_grad = (
        act_grad * up_value * gate_sigmoid * (1.0 + gate_value * (1.0 - gate_sigmoid))
    ).astype(BF)
    up_grad = (act_grad * gate_silu).astype(BF)
    down_terms = [
        contract(part, grad_own[:rows], 0, 0).astype(BF).reshape(2, 4, 4, ff // 64, half)
        for part in (activated[:rows], activated_far)
    ]
    down_far_terms = scatter_far(place, down_terms, "y", 1)
    orders = {axis: block_order(place, axis) for axis in AXES}
    gate_far = scatter_dot(orders["z"], after(second[:rows], gate_grad), gate_grad[:rows], "z", late=True)
    up_far = scatter_dot(orders["x"], after(second[:rows], up_grad), up_grad[:rows], "x", late=True)
    gate_grad, up_grad = after((gate_grad, up_grad), gate_far[3], up_far[3], down_far_terms[3])
    second_part = contract(gate_grad, gate_c, 1, 1) + contract(up_grad, up_c, 1, 1)
    gate_far = scatter_keep(gate_far, gate_grad[:rows], second_part)
    up_far = scatter_keep(up_far, up_grad[:rows], second_part)
    second_grad = second_part + swap_core(second_part)

    own_at = (core * length, 0)
    activated = after(activated[:rows], second_part)
    out_own = jnp.dot(activated, down_own, preferred_element_type=F32)
    out_far = jnp.dot(activated, down_far, preferred_element_type=F32)
    out_part = by_core(core, out_own, out_far, 1)
    got = swap_core(lax.dynamic_slice(out_part, ((1 - core) * length, 0), (length, d_model)))
    block_output = (
        lax.dynamic_slice(middle, own_at, (length, d_model))
        + lax.dynamic_slice(out_part, own_at, (length, d_model))
        + got
    ).astype(BF)

    middle_grad = grad_out.astype(F32) + norm_backward(
        scaled_two, inverse_two, gain_second, second_grad
    )
    gain_two_grad = jnp.sum((second_grad * scaled_two)[:rows], axis=0) * (core == 0).astype(F32)
    branch_grad = middle_grad.astype(BF)
    out_rows = lax.dynamic_slice(out_full, (core * half, 0), (half, d_model))
    gated_grad = contract(branch_grad, out_rows, 1, 1)
    out_right = lax.dynamic_slice(branch_grad, (0, core * half), (rows, half))
    convolved_grad = gated_grad * c_part
    c_grad = gated_grad * convolved
    from_one = taps[1] * lag_one * convolved_grad
    from_two = taps[2] * lag_two * convolved_grad
    convolved_grad, c_grad = convolved_grad[:rows], c_grad[:rows]
    product_grad = taps[0] * convolved_grad + from_one[1 : rows + 1] + from_two[2 : rows + 2]
    tap_grads = jnp.stack(
        [
            jnp.sum(convolved_grad * wide_product[:rows], axis=0),
            jnp.sum(convolved_grad * lagged_one[:rows], axis=0),
            jnp.sum(convolved_grad * lagged_two[:rows], axis=0),
        ]
    )
    c_grad = c_grad.astype(BF)
    grad_a = jnp.concatenate([(product_grad * x_part[:rows]).astype(BF), c_grad[:, :quarter]], axis=1)
    grad_b = jnp.concatenate([c_grad[:, quarter:], (product_grad * b_part[:rows]).astype(BF)], axis=1)
    gate_pass = scatter_pass(gate_far)
    up_pass = scatter_pass(up_far)
    down_pass = scatter_pass(down_far_terms)
    gate_sum = scatter_near(*gate_far, gate_pass, "z").astype(BF)
    up_sum = scatter_near(*up_far, up_pass, "x").astype(BF)
    down_sum = scatter_near(*down_far_terms, down_pass, "y").astype(BF)
    down_sum = jnp.where(core == 0, down_sum, down_sum[::-1])
    down_sum = down_sum.reshape(4, 4, ff // 64, half)
    normed_part = contract(grad_a, in_a, 1, 1) + contract(grad_b, in_b, 1, 1)
    gain_one_grad = jnp.sum(normed_part * scaled_one[:rows], axis=0)
    tap_full = lax.dynamic_update_slice(
        jnp.zeros((3, d_model), F32), tap_grads, (0, core * half)
    )
    extra = jnp.concatenate(
        [gain_one_grad[None], tap_full, gain_two_grad[None], jnp.zeros((123, d_model), F32)]
    ).astype(BF)
    left_b = after(normed[:rows], grad_b, up_pass)
    left_a = after(normed[:rows], gate_pass)
    left_c = after(gated_full[:rows], grad_b, down_pass)
    far_b = scatter_dot(orders["x"], left_b, grad_b, "x")
    far_a = scatter_dot(orders["z"], left_a, grad_a, "z", extra)
    far_c = scatter_dot(orders["y"], left_c, out_right, "y")
    far_a, far_b = ((after(far[0], down_pass, far_c[3]), *far[1:]) for far in (far_a, far_b))
    mix_b = scatter_near(*far_b, scatter_pass(far_b), "x").astype(BF)
    mix_a = scatter_near(*far_a, scatter_pass(far_a), "z").astype(BF)
    mix_c = scatter_near(*far_c, scatter_pass(far_c), "y").astype(BF)

    got = swap_core(lax.dynamic_slice(normed_part, ((1 - core) * length, 0), (length, d_model)))
    normed_grad = lax.dynamic_slice(normed_part, own_at, (length, d_model)) + got
    tokens_grad = (
        lax.dynamic_slice(middle_grad, own_at, (length, d_model))
        + norm_backward(
            lax.dynamic_slice(scaled_one, own_at, (length, d_model)),
            lax.dynamic_slice(inverse_one, own_at, (length, 1)),
            gain_first,
            normed_grad,
        )
    ).astype(BF)

    flow_a = jnp.concatenate([mix_a, gate_sum], axis=-1)
    flow_b = jnp.concatenate([mix_b, up_sum], axis=-1)
    flow_c = jnp.concatenate([mix_c, down_sum], axis=-2)
    trades = [("x", 0), ("y", 0), ("z", 1)]
    fars = [scatter_far(place, f, *at) for f, at in zip((flow_a, flow_b, flow_c), trades)]
    passes = [scatter_pass(far) for far in fars]
    flow_a, flow_b, flow_c = (
        after(scatter_near(*far, passing, at[0]).astype(BF), *passes)
        for far, passing, at in zip(fars, passes, trades)
    )
    flow_a = scatter_small(place, flow_a, "y")
    flow_b = scatter_small(place, flow_b, "z")
    flow_c = scatter_small(place, flow_c, "x")

    lead = own_rows // 2
    deep = (flow_c.shape[0] - own_rows) // 2

    def other_rows(flow, first, count):
        return swap_core(
            jnp.where(core == 0, flow[first + count : first + 2 * count], flow[first : first + count])
        )

    got = [
        other_rows(flow_a, 0, lead),
        other_rows(flow_b, 0, lead),
        other_rows(flow_c, 0, lead),
        other_rows(flow_c, own_rows, deep),
    ]
    in_grad, gate_grad, up_grad, out_grad, down_grad, norm_grad, tap_grad, ffn_norm_grad = finish(
        core, [flow_a, flow_b, flow_c, *got], half, ff_half
    )
    return (
        block_output,
        tokens_grad,
        norm_grad,
        in_grad,
        tap_grad,
        out_grad,
        ffn_norm_grad,
        gate_grad,
        up_grad,
        down_grad,
    )


def solution(mesh):
    return jax.shard_map(
        on_device,
        mesh=mesh,
        in_specs=(
            P("fsdp", None),
            P("fsdp"),
            P("fsdp", None),
            P(None, "fsdp"),
            P("fsdp", None),
            P("fsdp"),
            P("fsdp", None),
            P("fsdp", None),
            P("fsdp", None),
            P(),
            P("fsdp", None),
        ),
        out_specs=(
            P("fsdp", None),
            P("fsdp", None),
            P("fsdp"),
            P("fsdp", None),
            P(None, "fsdp"),
            P("fsdp", None),
            P("fsdp"),
            P("fsdp", None),
            P("fsdp", None),
            P("fsdp", None),
        ),
        check_vma=False,
    )
```
